256 devices in a mesh: grp: 16 (over y, x_hi, core), sh: 16 (over z, x_lo).
Axes of the slice: x: 4 (x_hi: 2, x_lo: 2; x = x_hi * 2 + x_lo), y: 4, z: 8, core: 2. Of those that a mesh axis runs over, the one named last changes fastest.
Arguments:
- factors: bfloat16 [48, 128, 14336], P('grp', None, 'sh'), may hold values from -0.5 to 0.5
- screen: int32 [48, 1, 112], P('grp', None, 'sh'), may hold values 0 or 1
- occ_energy: float32 [48], replicated, may hold values from -1.5 to -0.3
- virt_energy: float32 [128], replicated, may hold values from 0.5 to 3
Outputs:
- gamma: bfloat16 [48, 128, 14336], P('grp', 'sh')
The draws below stay inside these ranges and needn't reach their ends.
Inputs may be any that keep to these rules, and one draw needn't show every extreme that they name: `screen`: 1 keeps a block of 128 virtual by 128 auxiliary functions of one occupied orbital, 0 screens it out.
All inputs are finite; a program needn't handle non-finite values.
Results may differ from the reference program's by a relative error of at most 0.0049.
Values may be sent and summed in bfloat16 or wider, within the bound.
No kernel may reach another device: no remote copies, remote signals or barrier semaphores. Data moves between devices by JAX's collectives and lax.ppermute only.
A program may use at most 64 MiB of HBM per device.

```python
import jax
import jax.numpy as jnp
from jax import lax

VIRT = 128
BLK = 128
NAUX = 14336
OCC = 48


def plant(entries, rng, low, top_value):
    spot = [jax.random.randint(jax.random.fold_in(rng, axis), (), 0, length) for axis, length in enumerate(entries.shape)]
    main_axis = entries.shape.index(max(entries.shape))
    neighbour = spot[:main_axis] + [(spot[main_axis] + 1) % entries.shape[main_axis]] + spot[main_axis + 1:]
    return entries.at[tuple(spot)].set(low).at[tuple(neighbour)].set(top_value)


def shard_levels(own_key, dims, pieces, smallest, top_value):
    def one(axis_at, blocks):
        draws = jax.random.uniform(jax.random.fold_in(jax.random.fold_in(own_key, 6), axis_at), (blocks,), jnp.float32, smallest / len(pieces), top_value / len(pieces))
        return jnp.repeat(jnp.exp(draws), dims[axis_at] // blocks).reshape((-1,) + (1,) * (len(dims) - axis_at - 1))

    factor_of = one(*pieces[0])
    for cut in pieces[1:]:
        factor_of = factor_of * one(*cut)
    return factor_of


def centred(own_key, extent, deviation, most, cuts=(), dtype=jnp.bfloat16):
    factor_of = shard_levels(own_key, extent, cuts, -0.22, 0.18) if cuts else 1.0
    drawn = jax.random.normal(own_key, extent, jnp.float32) * deviation * factor_of
    return jnp.minimum(jnp.maximum(drawn, -most), most).astype(dtype)


def setup_inputs(seed: int = 0) -> dict:
    keys = jax.random.split(jax.random.key(seed), 5)
    factors = centred(keys[0], (OCC, VIRT, NAUX), 0.09, 0.5, ((0, 16), (2, 16)))
    screen = plant((jax.random.randint(keys[1], (OCC, VIRT // BLK, NAUX // BLK), 0, 4) < 3).astype(jnp.int32), jax.random.fold_in(keys[1], 1), 0, 1)
    occ_energy = jnp.clip(jax.random.uniform(keys[2], (OCC,), jnp.float32, -1.5, -0.3), -1.5, -0.3)
    virt_energy = jnp.clip(jax.random.uniform(keys[3], (VIRT,), jnp.float32, 0.5, 3.0), 0.5, 3.0)
    return {"factors": factors, "screen": screen, "occ_energy": occ_energy, "virt_energy": virt_energy}


def reference(factors, screen, occ_energy, virt_energy):
    occ_all, virt_width, aux_width = factors.shape
    wide_mask = jnp.repeat(jnp.repeat(screen, BLK, axis=1), BLK, axis=2)
    screened = (factors * wide_mask.astype(jnp.bfloat16)).reshape(occ_all * virt_width, aux_width)
    coulomb = lax.dot_general(screened, screened, (((1,), (1,)), ((), ())), preferred_element_type=jnp.float32)
    row_energy = (virt_energy[None, :] - occ_energy[:, None]).reshape(-1)
    amplitude = (coulomb / (row_energy[:, None] + row_energy[None, :])).astype(jnp.bfloat16)
    four_index = amplitude.reshape(occ_all, virt_width, occ_all, virt_width).astype(jnp.float32)
    combined = (2.0 * four_index - jnp.transpose(four_index, (0, 3, 2, 1))).astype(jnp.bfloat16)
    combined = combined.reshape(occ_all * virt_width, occ_all * virt_width)
    gamma = jnp.dot(combined, screened, preferred_element_type=jnp.float32).astype(jnp.bfloat16)
    return gamma.reshape(occ_all, virt_width, aux_width)
```

```python
import functools

import jax
import jax.numpy as jnp
from jax import lax
from jax.experimental import pallas as pl
from jax.experimental.pallas import tpu as pltpu
from jax.sharding import Mesh, PartitionSpec as P

BLK = 128
NY, NXH, NC, NZ, NXL = 4, 2, 2, 8, 2
GRP = ("y", "xh", "core")
SH = ("z", "xl")
X = ("xh", "xl")
BF = jnp.bfloat16
F32 = jnp.float32


def flip_x(value, bits):
    return lax.ppermute(value, X, [(i, i ^ bits) for i in range(NXH * NXL)])


def shift(value, axis, steps):
    count = lax.axis_size(axis)
    return lax.ppermute(value, axis, [(i, (i + steps) % count) for i in range(count)])


def flip_core(value):
    return lax.ppermute(value, "core", [(0, 1), (1, 0)])


def coulomb_kernel(same_ref, own, xlf, bof, xh0, xh1, *refs):
    out = refs[-1]
    near, far = refs[0:5], refs[5:10]
    hr = xh0.shape[0]

    def dot(a, b):
        return lax.dot_general(a[...], b[...], (((1,), (1,)), ((), ())), preferred_element_type=F32)

    def run(mine, other):
        def put(block, rows, left, right):
            columns = [(0, slice(0, 2 * hr), 0), (1, slice(0, 2 * hr), 1), (2, slice(0, hr), 2),
                       (2, slice(hr, 2 * hr), 3), (3, slice(0, 2 * hr), 4)]
            for d, cols, piece in columns:
                out[block + d, rows, cols] = dot(left, mine[piece]) + dot(right, other[piece])

        put(0, slice(0, 2 * hr), own, xlf)
        put(4, slice(0, hr), xh0, bof.at[pl.ds(0, hr)])
        put(4, slice(hr, 2 * hr), xh1, bof.at[pl.ds(hr, hr)])

    @pl.when(same_ref[0] == 1)
    def _():
        run(near, far)

    @pl.when(same_ref[0] == 0)
    def _():
        run(far, near)


def gamma_kernel(pos_ref, comb, *refs, base, wide):
    near, far, outs = refs[0:5], refs[5:10], refs[10:]
    half = near[0].shape[1]
    hr = near[2].shape[0]
    z, xl = pos_ref[0], pos_ref[1]
    for fl in range(2):
        h = lax.rem(xl + fl, 2)
        lhs = [comb[base + d, h] for d in range(NY)]
        parts = [lhs[0], lhs[1], lhs[2][:, :hr], lhs[2][:, hr:], lhs[3]]
        for k, pieces in enumerate((near, far)):
            acc = jnp.dot(parts[0], pieces[0][...], preferred_element_type=F32)
            for p in range(1, 5):
                acc += jnp.dot(parts[p], pieces[p][...], preferred_element_type=F32)
            rows = acc.shape[0] // NZ
            for zp in range(NZ):
                outs[fl][lax.rem(zp + NZ - z, NZ), :, k * half:(k + 1) * half] = acc[zp * rows:(zp + 1) * rows].astype(
                    outs[fl].dtype
                )


def assemble_kernel(pos_ref, *refs):
    out = refs[-1]
    z, core = pos_ref[0], pos_ref[2]
    half = refs[0].shape[1] // 2
    for k in range(NZ):
        source = lax.rem(z + NZ - k, NZ)
        for part in range(2):
            start = pl.multiple_of(source * 2 * half + lax.rem(core + part, 2) * half, 128)
            out[:, pl.ds(start, half)] = refs[k][:, part * half:(part + 1) * half]


def on_device(factors, screen, occ_energy, virt_energy):
    occ_g, virt, aux = factors.shape
    rows = occ_g * virt
    hr = rows // 2
    y, xh, c, z, xl = (lax.axis_index(n) for n in ("y", "xh", "core", "z", "xl"))
    wide_mask = jnp.repeat(jnp.repeat(screen, BLK, axis=1), BLK, axis=2)
    own = (factors * wide_mask.astype(BF)).reshape(rows, aux)

    with jax.named_scope("gather"):
        j0 = lax.ppermute(own, ("core", "xl"), [(0, 0), (1, 2), (2, 1), (3, 3)])
        xlf = flip_x(own, 1)
        bof = flip_x(own, 3)
        j1 = shift(j0, "y", 1)
        j3 = shift(j0, "y", -1)
        xh0 = flip_x(xlf[:hr], 3)
        xh1 = flip_x(bof[hr:], 1)
        j2a = shift(j1[:hr], "y", 1)
        j2b = shift(j3[hr:], "y", -1)
        near = [j0, j1, j2a, j2b, j3]
        far = [flip_core(p) for p in near]

    vmem = pl.BlockSpec(memory_space=pltpu.VMEM)
    smem = pl.BlockSpec(memory_space=pltpu.SMEM)
    with jax.named_scope("coulomb"):
        same = (xl == c).astype(jnp.int32).reshape(1)
        partial = pl.pallas_call(
            coulomb_kernel,
            out_shape=jax.ShapeDtypeStruct((NZ, rows, rows), F32),
            in_specs=[smem] + [vmem] * 15,
            out_specs=vmem,
            compiler_params=pltpu.CompilerParams(vmem_limit_bytes=48 << 20),
        )(same, own, xlf, bof, xh0, xh1, *near, *far)
        block = lax.psum_scatter(partial.reshape(NZ * rows, rows), "z", scatter_dimension=0, tiled=True)

    with jax.named_scope("combined"):
        e, d = z // NY, z % NY
        row_group = (y * NXH + (xh + e) % NXH) * NC + c
        col_group = (((y + NY - d) % NY) * NXH + xh) * NC + xl
        row_occ = lax.dynamic_slice_in_dim(occ_energy, row_group * occ_g, occ_g)
        col_occ = lax.dynamic_slice_in_dim(occ_energy, col_group * occ_g, occ_g)
        row_energy = (virt_energy[None, :] - row_occ[:, None]).reshape(-1)
        col_energy = (virt_energy[None, :] - col_occ[:, None]).reshape(-1)
        amplitude = (block / (row_energy[:, None] + col_energy[None, :])).astype(BF)
        four = amplitude.reshape(occ_g, virt, occ_g, virt).astype(F32)
        comb = (2.0 * four - jnp.transpose(four, (0, 3, 2, 1))).astype(BF)
        comb = comb.reshape(occ_g, NZ, NXL, virt // (NZ * NXL), rows)
        comb = jnp.transpose(comb, (2, 1, 0, 3, 4)).reshape(NXL, hr, rows)
        comb = lax.all_gather(comb, "z")

    with jax.named_scope("gamma"):
        pos = jnp.stack([z, xl, c]).astype(jnp.int32)
        piece = hr // NZ

        def gamma_of(base, types):
            return pl.pallas_call(
                functools.partial(gamma_kernel, base=base, wide=2 * aux),
                out_shape=[jax.ShapeDtypeStruct((NZ, piece, 2 * aux), t) for t in types],
                in_specs=[smem] + [vmem] * 11,
                out_specs=[vmem] * 2,
                compiler_params=pltpu.CompilerParams(vmem_limit_bytes=48 << 20),
            )(pos, comb, *near, *far)

        to_xh, to_both = gamma_of(NY, (BF, BF))
        from_both = flip_x(to_both, 3)
        from_xh = flip_x(to_xh, 2)
        mine, to_xl = gamma_of(0, (F32, BF))
        from_xl = flip_x(to_xl, 1)
        total = (mine + from_xl.astype(F32) + from_both.astype(F32) + from_xh.astype(F32)).astype(BF)

    with jax.named_scope("spread"):
        got = [total[0]] + [shift(total[k], "z", k) for k in range(1, NZ)]
        out = pl.pallas_call(
            assemble_kernel,
            out_shape=jax.ShapeDtypeStruct((piece, NZ * 2 * aux), BF),
            in_specs=[smem] + [vmem] * NZ,
            out_specs=vmem,
            compiler_params=pltpu.CompilerParams(vmem_limit_bytes=16 << 20),
        )(pos, *got)
    return out.reshape(occ_g, piece // occ_g, NZ * 2 * aux)


def solution(mesh):
    split = Mesh(mesh.devices.reshape(NY, NXH, NC, NZ, NXL), ("y", "xh", "core", "z", "xl"))
    placed = (P(GRP, None, SH), P(GRP, None, SH), P(), P())
    return jax.shard_map(on_device, mesh=split, in_specs=placed, out_specs=P(GRP, SH, None), check_vma=False)
```

```python
import functools

import jax
import jax.numpy as jnp
from jax import lax
from jax.experimental import pallas as pl
from jax.experimental.pallas import tpu as pltpu
from jax.sharding import Mesh, PartitionSpec as P

BLK = 128
NY, NXH, NC, NZ, NXL = 4, 2, 2, 8, 2
GRP = ("y", "xh", "core")
SH = ("z", "xl")
X = ("xh", "xl")
BF = jnp.bfloat16
F32 = jnp.float32


def flip_x(value, bits):
    return lax.ppermute(value, X, [(i, i ^ bits) for i in range(NXH * NXL)])


def shift(value, axis, steps):
    count = lax.axis_size(axis)
    return lax.ppermute(value, axis, [(i, (i + steps) % count) for i in range(count)])


def flip_core(value):
    return lax.ppermute(value, "core", [(0, 1), (1, 0)])


def units():
    first = [(0, d, jj) for d in (0, 1) for jj in range(3)] + [(0, 3, 0), (0, 3, 1)]
    second = [(0, 3, 2)] + [(0, 2, jj) for jj in range(3)] + [(1, d, jj) for d in range(NY) for jj in range(3)]
    return first, second


FIRST, SECOND = units()
PLACE = {u: (n, 0) for n, u in enumerate(FIRST)} | {u: (n // 2, 1 + n % 2) for n, u in enumerate(SECOND)}


def dot_t(a, b):
    return lax.dot_general(a, b, (((1,), (1,)), ((), ())), preferred_element_type=F32)


def first_kernel(pos_ref, own, xlf, n0, n1, n3, f0, f1, f3, *refs):
    outs, scr = refs[:NZ], refs[NZ]
    z = pos_ref[0]

    def run(mine, other):
        for d, piece in ((0, 0), (1, 1), (3, 2)):
            count = 2 if d == 3 else 3
            rows = pl.ds(0, count * BLK)
            got = dot_t(own[...], mine[piece][rows, :]) + dot_t(xlf[...], other[piece][rows, :])
            for jj in range(count):
                scr[PLACE[(0, d, jj)][0]] = got[:, jj * BLK:(jj + 1) * BLK]

    @pl.when(pos_ref[1] == pos_ref[2])
    def _():
        run((n0, n1, n3), (f0, f1, f3))

    @pl.when(pos_ref[1] != pos_ref[2])
    def _():
        run((f0, f1, f3), (n0, n1, n3))

    for k in range(NZ):
        outs[k][...] = scr[lax.rem(z + k, NZ)].astype(outs[k].dtype)


def second_kernel(pos_ref, own, xlf, bof, xh0, xh1, *refs):
    near, far, outs, scr = refs[0:5], refs[5:10], refs[10:10 + NZ], refs[10 + NZ]
    z = pos_ref[0]
    hr = xh0.shape[0]

    def run(mine, other):
        def put(e, d, left, right, row0, col0, a, b):
            got = dot_t(left, a) + dot_t(right, b)
            width = got.shape[1]
            at = col0
            while at < col0 + width:
                jj = at // BLK
                end = min((jj + 1) * BLK, col0 + width)
                n, slot = PLACE[(e, d, jj)]
                if slot:
                    scr[n, slot - 1, row0:row0 + got.shape[0], at - jj * BLK:end - jj * BLK] = got[:, at - col0:end - col0]
                at = end

        put(0, 3, own[...], xlf[...], 0, 2 * BLK, mine[4][pl.ds(2 * BLK, BLK), :], other[4][pl.ds(2 * BLK, BLK), :])
        for e, left, right, row0 in (
            (0, own[...], xlf[...], 0),
            (1, xh0[...], bof[pl.ds(0, hr), :], 0),
            (1, xh1[...], bof[pl.ds(hr, hr), :], hr),
        ):
            for d, col0, piece in ((0, 0, 0), (1, 0, 1), (2, 0, 2), (2, hr, 3), (3, 0, 4)):
                if e == 1 or d == 2:
                    put(e, d, left, right, row0, col0, mine[piece][...], other[piece][...])

    @pl.when(pos_ref[1] == pos_ref[2])
    def _():
        run(near, far)

    @pl.when(pos_ref[1] != pos_ref[2])
    def _():
        run(far, near)

    for k in range(NZ):
        outs[k][...] = scr[lax.rem(z + k, NZ)].astype(outs[k].dtype)


def combined_kernel(pos_ref, occ_ref, v_col, v_row, *refs):
    one, two, out, scr = refs[:NZ], refs[NZ:2 * NZ], refs[2 * NZ], refs[2 * NZ + 1]
    virt = v_row.shape[1]
    count = out.shape[2] // (NZ * 8)
    for slot in range(3):
        e, col_occ, row_occ = pos_ref[3 + 3 * slot], pos_ref[4 + 3 * slot], pos_ref[5 + 3 * slot]
        del e
        col = v_row[...] - occ_ref[col_occ]
        for i in range(count):
            rows = pl.ds(i * virt, virt)
            if slot == 0:
                parts = [r[rows, :] for r in one]
            else:
                parts = [r[slot - 1, rows, :] for r in two]
            total = parts[0]
            for part in parts[1:]:
                total = total + part.astype(F32)
            row = v_col[...] - occ_ref[row_occ + i]
            amp = (total / (row + col)).astype(BF).astype(F32)
            comb = 2.0 * amp - amp.T
            for zp in range(NZ):
                for h in range(NXL):
                    at = (zp * NXL + h) * 8
                    scr[h, (zp * count + i) * 8:(zp * count + i + 1) * 8, :] = comb[at:at + 8]
        for h in range(NXL):
            out[slot, h] = scr[h].astype(BF)


def gamma_kernel(pos_ref, *refs, group):
    combs, near, far, outs, scr = refs[0:9], refs[9:14], refs[14:19], refs[19:21], refs[21]
    half = near[0].shape[1]
    hr = near[2].shape[0]
    z, xl = pos_ref[0], pos_ref[1]
    for ref, step in zip(combs[:7], (0, 1, -1, 2, -2, 3, -3)):
        scr[lax.rem(z + NZ - step, NZ)] = ref[...]
    opposite = lax.rem(z + NZ // 2, NZ)
    part = combs[7].shape[2]
    scr[opposite, :, :, 0:part, :] = combs[7][...]
    scr[opposite, :, :, part:2 * part, :] = combs[8][...]
    for fl in range(2):
        h = lax.rem(xl + fl, 2)
        lhs = []
        for d in range(NY):
            cols = [scr[PLACE[(group, d, jj)][0], PLACE[(group, d, jj)][1], h] for jj in range(3)]
            lhs.append(jnp.concatenate(cols, axis=1))
        parts = [lhs[0], lhs[1], lhs[2][:, :hr], lhs[2][:, hr:], lhs[3]]
        for k, pieces in enumerate((near, far)):
            acc = jnp.dot(parts[0], pieces[0][...], preferred_element_type=F32)
            for p in range(1, 5):
                acc += jnp.dot(parts[p], pieces[p][...], preferred_element_type=F32)
            rows = acc.shape[0] // NZ
            for zp in range(NZ):
                outs[fl][lax.rem(zp + NZ - z, NZ), :, k * half:(k + 1) * half] = acc[zp * rows:(zp + 1) * rows].astype(
                    outs[fl].dtype
                )


def assemble_kernel(pos_ref, *refs):
    out = refs[-1]
    z, core = pos_ref[0], pos_ref[2]
    half = refs[0].shape[1] // 2
    for k in range(NZ):
        source = lax.rem(z + NZ - k, NZ)
        for part in range(2):
            start = pl.multiple_of(source * 2 * half + lax.rem(core + part, 2) * half, 128)
            out[:, pl.ds(start, half)] = refs[k][:, part * half:(part + 1) * half]


def on_device(factors, screen, occ_energy, virt_energy):
    occ_g, virt, aux = factors.shape
    rows = occ_g * virt
    hr = rows // 2
    y, xh, c, z, xl = (lax.axis_index(n) for n in ("y", "xh", "core", "z", "xl"))
    wide_mask = jnp.repeat(jnp.repeat(screen, BLK, axis=1), BLK, axis=2)
    own = (factors * wide_mask.astype(BF)).reshape(rows, aux)

    with jax.named_scope("gather"):
        j0 = lax.ppermute(own, ("core", "xl"), [(0, 0), (1, 2), (2, 1), (3, 3)])
        xlf = flip_x(own, 1)
        bof = flip_x(own, 3)
        j1 = shift(j0, "y", 1)
        j3 = shift(j0, "y", -1)
        xh0 = flip_x(xlf[:hr], 3)
        xh1 = flip_x(bof[hr:], 1)
        j2a = shift(j1[:hr], "y", 1)
        j2b = shift(j3[hr:], "y", -1)
        near = [j0, j1, j2a, j2b, j3]
        far = [flip_core(p) for p in near]

    vmem = pl.BlockSpec(memory_space=pltpu.VMEM)
    smem = pl.BlockSpec(memory_space=pltpu.SMEM)
    params = pltpu.CompilerParams(vmem_limit_bytes=48 << 20)
    pos = [z, xl, c]
    table = jnp.array([[FIRST[n], SECOND[2 * n], SECOND[2 * n + 1]] for n in range(NZ)], jnp.int32)
    here = lax.dynamic_index_in_dim(table, z, 0, keepdims=False)
    for slot in range(3):
        e, d, jj = here[slot, 0], here[slot, 1], here[slot, 2]
        row_group = (y * NXH + (xh + e) % NXH) * NC + c
        col_group = (((y + NY - d) % NY) * NXH + xh) * NC + xl
        pos += [e, col_group * occ_g + jj, row_group * occ_g]
    pos = jnp.stack(pos).astype(jnp.int32)

    def exchanged(parts):
        return [parts[0]] + [shift(parts[k], "z", k) for k in range(1, NZ)]

    with jax.named_scope("coulomb"):
        first = pl.pallas_call(
            first_kernel,
            out_shape=[jax.ShapeDtypeStruct((rows, BLK), BF if k else F32) for k in range(NZ)],
            in_specs=[smem] + [vmem] * 8,
            out_specs=[vmem] * NZ,
            scratch_shapes=[pltpu.VMEM((NZ, rows, BLK), F32)],
            compiler_params=params,
        )(pos, own, xlf, near[0], near[1], near[4], far[0], far[1], far[4])
        first = exchanged(first)
        second = pl.pallas_call(
            second_kernel,
            out_shape=[jax.ShapeDtypeStruct((2, rows, BLK), BF if k else F32) for k in range(NZ)],
            in_specs=[smem] + [vmem] * 15,
            out_specs=[vmem] * NZ,
            scratch_shapes=[pltpu.VMEM((NZ, 2, rows, BLK), F32)],
            compiler_params=params,
        )(pos, own, xlf, bof, xh0, xh1, *near, *far)
        second = exchanged(second)

    with jax.named_scope("combined"):
        comb = pl.pallas_call(
            combined_kernel,
            out_shape=jax.ShapeDtypeStruct((3, NXL, hr, BLK), BF),
            in_specs=[smem, smem] + [vmem] * (2 + 2 * NZ),
            out_specs=vmem,
            scratch_shapes=[pltpu.VMEM((NXL, hr, BLK), F32)],
            compiler_params=params,
        )(pos, occ_energy, virt_energy[:, None], virt_energy[None, :], *first, *second)
        up1, down1 = shift(comb, "z", 1), shift(comb, "z", -1)
        up2, down2 = shift(up1, "z", 1), shift(down1, "z", -1)
        up3, down3 = shift(up2, "z", 1), shift(down2, "z", -1)
        up4, down4 = shift(up3[:, :, :hr // 2], "z", 1), shift(down3[:, :, hr // 2:], "z", -1)
        combs = [comb, up1, down1, up2, down2, up3, down3, up4, down4]

    with jax.named_scope("gamma"):
        piece = hr // NZ

        def gamma_of(group, types):
            return pl.pallas_call(
                functools.partial(gamma_kernel, group=group),
                out_shape=[jax.ShapeDtypeStruct((NZ, piece, 2 * aux), t) for t in types],
                in_specs=[smem] + [vmem] * 19,
                out_specs=[vmem] * 2,
                scratch_shapes=[pltpu.VMEM((NZ, 3, NXL, hr, BLK), BF)],
                compiler_params=params,
            )(pos, *combs, *near, *far)

        to_xh, to_both = gamma_of(1, (BF, BF))
        from_both = flip_x(to_both, 3)
        from_xh = flip_x(to_xh, 2)
        mine, to_xl = gamma_of(0, (F32, BF))
        from_xl = flip_x(to_xl, 1)
        total = (mine + from_xl.astype(F32) + from_both.astype(F32) + from_xh.astype(F32)).astype(BF)

    with jax.named_scope("spread"):
        got = [total[0]] + [shift(total[k], "z", k) for k in range(1, NZ)]
        out = pl.pallas_call(
            assemble_kernel,
            out_shape=jax.ShapeDtypeStruct((piece, NZ * 2 * aux), BF),
            in_specs=[smem] + [vmem] * NZ,
            out_specs=vmem,
            compiler_params=pltpu.CompilerParams(vmem_limit_bytes=16 << 20),
        )(pos, *got)
    return out.reshape(occ_g, piece // occ_g, NZ * 2 * aux)


def solution(mesh):
    split = Mesh(mesh.devices.reshape(NY, NXH, NC, NZ, NXL), ("y", "xh", "core", "z", "xl"))
    placed = (P(GRP, None, SH), P(GRP, None, SH), P(), P())
    return jax.shard_map(on_device, mesh=split, in_specs=placed, out_specs=P(GRP, SH, None), check_vma=False)
```

```python
import functools

import jax
import jax.numpy as jnp
from jax import lax
from jax.experimental import pallas as pl
from jax.experimental.pallas import tpu as pltpu
from jax.sharding import Mesh, PartitionSpec as P

BLK = 128
NY, NXH, NC, NZ, NXL = 4, 2, 2, 8, 2
GRP = ("y", "xh", "core")
SH = ("z", "xl")
X = ("xh", "xl")
BF = jnp.bfloat16
F32 = jnp.float32


def flip_x(value, bits):
    return lax.ppermute(value, X, [(i, i ^ bits) for i in range(NXH * NXL)])


def shift(value, axis, steps):
    count = lax.axis_size(axis)
    return lax.ppermute(value, axis, [(i, (i + steps) % count) for i in range(count)])


def flip_core(value):
    return lax.ppermute(value, "core", [(0, 1), (1, 0)])


def units():
    first = [(0, d, jj) for d in (0, 1) for jj in range(3)] + [(0, 3, 0), (0, 3, 1)]
    second = [(0, 3, 2)] + [(0, 2, jj) for jj in range(3)] + [(1, d, jj) for d in range(NY) for jj in range(3)]
    return first, second


FIRST, SECOND = units()
PLACE = {u: (n, 0) for n, u in enumerate(FIRST)} | {u: (n // 2, 1 + n % 2) for n, u in enumerate(SECOND)}


def dot_t(a, b):
    return lax.dot_general(a, b, (((1,), (1,)), ((), ())), preferred_element_type=F32)


def emit(outs, scr, z, cut):
    for k in range(NZ):
        part = scr.at[lax.rem(z + k, NZ)]
        if k == 4:
            outs[4][...] = part[cut[0]].astype(BF)
            outs[8][...] = part[cut[1]].astype(BF)
        else:
            outs[k][...] = part[...]


def first_kernel(own, xlf, n0, n1, n3, f0, f1, f3, *refs):
    outs, scr = refs[:NZ + 1], refs[NZ + 1]
    z, xl, c = lax.axis_index("z"), lax.axis_index("xl"), lax.axis_index("core")

    def run(mine, other):
        for d, piece in ((0, 0), (1, 1), (3, 2)):
            count = 2 if d == 3 else 3
            rows = pl.ds(0, count * BLK)
            got = dot_t(own[...], mine[piece][rows, :]) + dot_t(xlf[...], other[piece][rows, :])
            for jj in range(count):
                scr[PLACE[(0, d, jj)][0]] = got[:, jj * BLK:(jj + 1) * BLK]

    @pl.when(xl == c)
    def _():
        run((n0, n1, n3), (f0, f1, f3))

    @pl.when(xl != c)
    def _():
        run((f0, f1, f3), (n0, n1, n3))

    half = own.shape[0] // 2
    emit(outs, scr, z, (slice(0, half), slice(half, 2 * half)))


def second_kernel(own, xlf, bof, xh0, xh1, *refs):
    near, far, outs, scr = refs[0:5], refs[5:10], refs[10:11 + NZ], refs[11 + NZ]
    z, xl, c = lax.axis_index("z"), lax.axis_index("xl"), lax.axis_index("core")
    hr = xh0.shape[0]

    def run(mine, other):
        def put(e, d, left, right, row0, col0, a, b):
            got = dot_t(left, a) + dot_t(right, b)
            width = got.shape[1]
            at = col0
            while at < col0 + width:
                jj = at // BLK
                end = min((jj + 1) * BLK, col0 + width)
                n, slot = PLACE[(e, d, jj)]
                if slot:
                    scr[n, slot - 1, row0:row0 + got.shape[0], at - jj * BLK:end - jj * BLK] = got[:, at - col0:end - col0]
                at = end

        put(0, 3, own[...], xlf[...], 0, 2 * BLK, mine[4][pl.ds(2 * BLK, BLK), :], other[4][pl.ds(2 * BLK, BLK), :])
        for e, left, right, row0 in (
            (0, own[...], xlf[...], 0),
            (1, xh0[...], bof[pl.ds(0, hr), :], 0),
            (1, xh1[...], bof[pl.ds(hr, hr), :], hr),
        ):
            for d, col0, piece in ((0, 0, 0), (1, 0, 1), (2, 0, 2), (2, hr, 3), (3, 0, 4)):
                if e == 1 or d == 2:
                    put(e, d, left, right, row0, col0, mine[piece][...], other[piece][...])

    @pl.when(xl == c)
    def _():
        run(near, far)

    @pl.when(xl != c)
    def _():
        run(far, near)

    emit(outs, scr, z, (0, 1))


def pick(z, values):
    out = jnp.int32(values[0])
    for n in range(1, NZ):
        out = jnp.where(z == n, jnp.int32(values[n]), out)
    return out


def combined_kernel(occ_ref, v_col, v_row, *refs):
    one, two, out, scr = refs[:3], refs[3:6], refs[6], refs[7]
    y, xh, c, z, xl = (lax.axis_index(n) for n in ("y", "xh", "core", "z", "xl"))
    virt = v_row.shape[1]
    count = out.shape[2] // (NZ * 8)
    for slot in range(3):
        unit = [FIRST[n] if slot == 0 else SECOND[2 * n + slot - 1] for n in range(NZ)]
        e, d, jj = (pick(z, [u[p] for u in unit]) for p in range(3))
        row_occ = ((y * NXH + lax.rem(xh + e, NXH)) * NC + c) * count
        col_occ = ((lax.rem(y + NY - d, NY) * NXH + xh) * NC + xl) * count + jj
        col = v_row[...] - occ_ref[col_occ]
        for i in range(count):
            rows = pl.ds(i * virt, virt)
            if slot == 0:
                parts = [r[rows, :] for r in one]
            else:
                parts = [r[slot - 1, rows, :] for r in two]
            total = parts[0] + parts[1].astype(F32) + parts[2].astype(F32)
            row = v_col[...] - occ_ref[row_occ + i]
            amp = (total / (row + col)).astype(BF).astype(F32)
            comb = 2.0 * amp - amp.T
            for zp in range(NZ):
                for h in range(NXL):
                    at = (zp * NXL + h) * 8
                    scr[h, (zp * count + i) * 8:(zp * count + i + 1) * 8, :] = comb[at:at + 8]
        for h in range(NXL):
            out[slot, h] = scr[h].astype(BF)


def gamma_kernel(*refs, group):
    combs, near, far, outs, scr = refs[0:9], refs[9:14], refs[14:19], refs[19:21], refs[21]
    half = near[0].shape[1]
    hr = near[2].shape[0]
    z, xl = lax.axis_index("z"), lax.axis_index("xl")
    for ref, step in zip(combs[:7], (0, 1, -1, 2, -2, 3, -3)):
        scr[lax.rem(z + NZ - step, NZ)] = ref[...]
    opposite = lax.rem(z + NZ // 2, NZ)
    part = combs[7].shape[2]
    scr[opposite, :, :, 0:part, :] = combs[7][...]
    scr[opposite, :, :, part:2 * part, :] = combs[8][...]
    for fl in range(2):
        h = lax.rem(xl + fl, 2)
        lhs = []
        for d in range(NY):
            cols = [scr[PLACE[(group, d, jj)][0], PLACE[(group, d, jj)][1], h] for jj in range(3)]
            lhs.append(jnp.concatenate(cols, axis=1))
        parts = [lhs[0], lhs[1], lhs[2][:, :hr], lhs[2][:, hr:], lhs[3]]
        for k, pieces in enumerate((near, far)):
            acc = jnp.dot(parts[0], pieces[0][...], preferred_element_type=F32)
            for p in range(1, 5):
                acc += jnp.dot(parts[p], pieces[p][...], preferred_element_type=F32)
            rows = acc.shape[0] // NZ
            for zp in range(NZ):
                outs[fl][lax.rem(zp + NZ - z, NZ), :, k * half:(k + 1) * half] = acc[zp * rows:(zp + 1) * rows].astype(
                    outs[fl].dtype
                )


def assemble_kernel(*refs):
    out = refs[-1]
    z, core = lax.axis_index("z"), lax.axis_index("core")
    half = refs[0].shape[1] // 2
    for k in range(NZ):
        source = lax.rem(z + NZ - k, NZ)
        for part in range(2):
            start = pl.multiple_of(source * 2 * half + lax.rem(core + part, 2) * half, 128)
            out[:, pl.ds(start, half)] = refs[k][:, part * half:(part + 1) * half]


def on_device(factors, screen, occ_energy, virt_energy):
    occ_g, virt, aux = factors.shape
    rows = occ_g * virt
    hr = rows // 2
    wide_mask = jnp.repeat(jnp.repeat(screen, BLK, axis=1), BLK, axis=2)
    own = (factors * wide_mask.astype(BF)).reshape(rows, aux)

    with jax.named_scope("gather"):
        j0 = lax.ppermute(own, ("core", "xl"), [(0, 0), (1, 2), (2, 1), (3, 3)])
        xlf = flip_x(own, 1)
        bof = flip_x(own, 3)
        j1 = shift(j0, "y", 1)
        j3 = shift(j0, "y", -1)
        xlf, bof, j1, j3 = lax.optimization_barrier((xlf, bof, j1, j3))
        xh0 = flip_x(xlf[:hr], 3)
        xh1 = flip_x(bof[hr:], 1)
        j2a = shift(j1[:hr], "y", 1)
        j2b = shift(j3[hr:], "y", -1)
        near = [j0, j1, j2a, j2b, j3]
        far = [flip_core(p) for p in near]

    vmem = pl.BlockSpec(memory_space=pltpu.VMEM)
    smem = pl.BlockSpec(memory_space=pltpu.SMEM)
    params = pltpu.CompilerParams(vmem_limit_bytes=48 << 20)

    def ring(parts):
        a, b = parts[4], parts[8]
        up, down = shift(a, "z", 1), shift(b, "z", -1)
        if a.shape == parts[0].shape[1:]:
            up = jnp.stack([up.astype(F32) + parts[3][0], parts[3][1]])
            down = jnp.stack([parts[5][0], down.astype(F32) + parts[5][1]])
        else:
            half = a.shape[0]
            up = jnp.concatenate([up.astype(F32) + parts[3][:half], parts[3][half:]])
            down = jnp.concatenate([parts[5][:half], down.astype(F32) + parts[5][half:]])
        up, down = shift(up.astype(BF), "z", 1), shift(down.astype(BF), "z", -1)
        for k in (2, 1):
            up, down = up.astype(F32) + parts[k], down.astype(F32) + parts[NZ - k]
            up, down = shift(up.astype(BF), "z", 1), shift(down.astype(BF), "z", -1)
        return [parts[0], up, down]

    def shapes(whole, half):
        full = [jax.ShapeDtypeStruct(whole, F32)] * NZ
        return full[:4] + [jax.ShapeDtypeStruct(half, BF)] + full[5:] + [jax.ShapeDtypeStruct(half, BF)]

    with jax.named_scope("coulomb"):
        first = pl.pallas_call(
            first_kernel,
            out_shape=shapes((rows, BLK), (hr, BLK)),
            in_specs=[vmem] * 8,
            out_specs=[vmem] * (NZ + 1),
            scratch_shapes=[pltpu.VMEM((NZ, rows, BLK), F32)],
            compiler_params=params,
        )(own, xlf, near[0], near[1], near[4], far[0], far[1], far[4])
        first = ring(first)
        second = pl.pallas_call(
            second_kernel,
            out_shape=shapes((2, rows, BLK), (rows, BLK)),
            in_specs=[vmem] * 15,
            out_specs=[vmem] * (NZ + 1),
            scratch_shapes=[pltpu.VMEM((NZ, 2, rows, BLK), F32)],
            compiler_params=params,
        )(own, xlf, bof, xh0, xh1, *near, *far)
        second = ring(second)

    with jax.named_scope("combined"):
        comb = pl.pallas_call(
            combined_kernel,
            out_shape=jax.ShapeDtypeStruct((3, NXL, hr, BLK), BF),
            in_specs=[smem] + [vmem] * 8,
            out_specs=vmem,
            scratch_shapes=[pltpu.VMEM((NXL, hr, BLK), F32)],
            compiler_params=params,
        )(occ_energy, virt_energy[:, None], virt_energy[None, :], *first, *second)
        up1, down1 = shift(comb, "z", 1), shift(comb, "z", -1)
        up2, down2 = shift(up1, "z", 1), shift(down1, "z", -1)
        up3, down3 = shift(up2, "z", 1), shift(down2, "z", -1)
        up4, down4 = shift(up3[:, :, :hr // 2], "z", 1), shift(down3[:, :, hr // 2:], "z", -1)
        combs = [comb, up1, down1, up2, down2, up3, down3, up4, down4]

    with jax.named_scope("gamma"):
        piece = hr // NZ

        def gamma_of(group, types):
            return pl.pallas_call(
                functools.partial(gamma_kernel, group=group),
                out_shape=[jax.ShapeDtypeStruct((NZ, piece, 2 * aux), t) for t in types],
                in_specs=[vmem] * 19,
                out_specs=[vmem] * 2,
                scratch_shapes=[pltpu.VMEM((NZ, 3, NXL, hr, BLK), BF)],
                compiler_params=params,
            )(*combs, *near, *far)

        to_xh, to_both = gamma_of(1, (BF, BF))
        from_both = flip_x(to_both, 3)
        from_xh = flip_x(to_xh, 2)
        mine, to_xl = gamma_of(0, (F32, BF))
        from_xl = flip_x(to_xl, 1)
        total = (mine + from_xl.astype(F32) + from_both.astype(F32) + from_xh.astype(F32)).astype(BF)

    with jax.named_scope("spread"):
        got = [total[0]] + [shift(total[k], "z", k) for k in range(1, NZ)]
        out = pl.pallas_call(
            assemble_kernel,
            out_shape=jax.ShapeDtypeStruct((piece, NZ * 2 * aux), BF),
            in_specs=[vmem] * NZ,
            out_specs=vmem,
            compiler_params=pltpu.CompilerParams(vmem_limit_bytes=16 << 20),
        )(*got)
    return out.reshape(occ_g, piece // occ_g, NZ * 2 * aux)


def solution(mesh):
    split = Mesh(mesh.devices.reshape(NY, NXH, NC, NZ, NXL), ("y", "xh", "core", "z", "xl"))
    placed = (P(GRP, None, SH), P(GRP, None, SH), P(), P())
    return jax.shard_map(on_device, mesh=split, in_specs=placed, out_specs=P(GRP, SH, None), check_vma=False)
```

```python
import functools

import jax
import jax.numpy as jnp
from jax import lax
from jax.experimental import pallas as pl
from jax.experimental.pallas import tpu as pltpu
from jax.sharding import Mesh, PartitionSpec as P

BLK = 128
NY, NXH, NC, NZ, NXL = 4, 2, 2, 8, 2
GRP = ("y", "xh", "core")
SH = ("z", "xl")
X = ("xh", "xl")
BF = jnp.bfloat16
F32 = jnp.float32


def flip_x(value, bits):
    return lax.ppermute(value, X, [(i, i ^ bits) for i in range(NXH * NXL)])


def shift(value, axis, steps):
    count = lax.axis_size(axis)
    return lax.ppermute(value, axis, [(i, (i + steps) % count) for i in range(count)])


def flip_core(value):
    return lax.ppermute(value, "core", [(0, 1), (1, 0)])


def dot_t(a, b):
    return lax.dot_general(a, b, (((1,), (1,)), ((), ())), preferred_element_type=F32)


def coulomb_kernel(own, xlf, bof0, bof1, xh0, xh1, *refs):
    near, far, out = refs[0:5], refs[5:10], refs[10]
    z, xl, c = lax.axis_index("z"), lax.axis_index("xl"), lax.axis_index("core")
    hr = xh0.shape[0]
    low, high, full = slice(0, hr), slice(hr, 2 * hr), slice(0, 2 * hr)

    def run(mine, other, xlf):
        for e, rows, left, right in (
            (0, full, own[...], xlf[...]),
            (1, low, xh0[...], bof0[...]),
            (1, high, xh1[...], bof1[...]),
        ):
            for d, cols, piece in ((0, full, 0), (1, full, 1), (2, low, 2), (2, high, 3), (3, full, 4)):
                at = lax.rem(e * NY + d + NZ - z, NZ)
                out[at, rows, cols] = dot_t(left, mine[piece][...]) + dot_t(right, other[piece][...])

    @pl.when(xl == c)
    def _():
        run(near, far, far[0])

    @pl.when(xl != c)
    def _():
        run(far, near, xlf)


def combined_kernel(occ_ref, v_col, v_row, mine, up, down, out, scr):
    y, xh, c, z, xl = (lax.axis_index(n) for n in ("y", "xh", "core", "z", "xl"))
    virt = v_row.shape[1]
    count = mine.shape[0] // virt
    e, d = z // NY, lax.rem(z, NY)
    row_occ = ((y * NXH + lax.rem(xh + e, NXH)) * NC + c) * count
    col_occ = ((lax.rem(y + NY - d, NY) * NXH + xh) * NC + xl) * count
    for i in range(count):
        for j in range(count):
            tile = (pl.ds(i * virt, virt), pl.ds(j * virt, virt))
            total = mine[tile] + up[tile].astype(F32) + down[tile].astype(F32)
            row, col = v_col[...] - occ_ref[row_occ + i], v_row[...] - occ_ref[col_occ + j]
            amp = (total / (row + col)).astype(BF).astype(F32)
            comb = 2.0 * amp - amp.T
            for zp in range(NZ):
                for h in range(NXL):
                    at = (zp * NXL + h) * 8
                    scr[h, (zp * count + i) * 8:(zp * count + i + 1) * 8, j * virt:(j + 1) * virt] = comb[at:at + 8]
    for h in range(NXL):
        out[h] = scr[h].astype(BF)


def gamma_kernel(*refs, group):
    combs, near, far, outs, scr = refs[0:9], refs[9:14], refs[14:19], refs[19:21], refs[21]
    half = near[0].shape[1]
    hr = near[2].shape[0]
    z, xl = lax.axis_index("z"), lax.axis_index("xl")
    for ref, step in zip(combs[:7], (0, 1, -1, 2, -2, 3, -3)):
        scr[lax.rem(z + NZ - step, NZ)] = ref[...]
    opposite = lax.rem(z + NZ // 2, NZ)
    part = combs[7].shape[1]
    scr[opposite, :, 0:part, :] = combs[7][...]
    scr[opposite, :, part:2 * part, :] = combs[8][...]
    for fl in range(2):
        h = lax.rem(xl + fl, 2)
        lhs = [scr[group * NY + d, h] for d in range(NY)]
        parts = [lhs[0], lhs[1], lhs[2][:, :hr], lhs[2][:, hr:], lhs[3]]
        for k, pieces in enumerate((near, far)):
            acc = jnp.dot(parts[0], pieces[0][...], preferred_element_type=F32)
            for p in range(1, 5):
                acc += jnp.dot(parts[p], pieces[p][...], preferred_element_type=F32)
            rows = acc.shape[0] // NZ
            for zp in range(NZ):
                outs[fl][lax.rem(zp + NZ - z, NZ), :, k * half:(k + 1) * half] = acc[zp * rows:(zp + 1) * rows].astype(
                    outs[fl].dtype
                )


def assemble_kernel(*refs):
    out = refs[-1]
    z, core = lax.axis_index("z"), lax.axis_index("core")
    half = refs[0].shape[1] // 2
    for k in range(NZ):
        source = lax.rem(z + NZ - k, NZ)
        for part in range(2):
            start = pl.multiple_of(source * 2 * half + lax.rem(core + part, 2) * half, 128)
            out[:, pl.ds(start, half)] = refs[k][:, part * half:(part + 1) * half]


def on_device(factors, screen, occ_energy, virt_energy):
    occ_g, virt, aux = factors.shape
    rows = occ_g * virt
    hr = rows // 2
    wide_mask = jnp.repeat(jnp.repeat(screen, BLK, axis=1), BLK, axis=2)
    own = (factors * wide_mask.astype(BF)).reshape(rows, aux)

    with jax.named_scope("gather"):
        same = lax.axis_index("xl") == lax.axis_index("core")
        j0 = lax.ppermute(own, ("core", "xl"), [(0, 0), (1, 2), (2, 1), (3, 3)])
        bof1 = flip_x(own[hr:], 3)
        j0, bof1, own_b = lax.optimization_barrier((j0, bof1, own))
        f0 = flip_core(j0)
        j1 = shift(j0, "y", 1)
        j3 = shift(j0, "y", -1)
        own_b, f0 = lax.optimization_barrier((own_b, f0))
        xlf = lax.ppermute(own_b, ("core", "xl"), [(0, 1), (3, 2)])
        bof0 = flip_x(own_b[:hr], 3)
        xh1 = flip_x(bof1, 1)
        j1, j3, xlf, bof0, xh1 = lax.optimization_barrier((j1, j3, xlf, bof0, xh1))
        xh0 = flip_x(jnp.where(same, f0[:hr], xlf[:hr]), 3)
        j2a = shift(j1[:hr], "y", 1)
        j2b = shift(j3[hr:], "y", -1)
        f1, f3 = flip_core(j1), flip_core(j3)
        near = [j0, j1, j2a, j2b, j3]
        far = [f0, f1, flip_core(j2a), flip_core(j2b), f3]

    vmem = pl.BlockSpec(memory_space=pltpu.VMEM)
    smem = pl.BlockSpec(memory_space=pltpu.SMEM)
    params = pltpu.CompilerParams(vmem_limit_bytes=48 << 20)

    with jax.named_scope("coulomb"):
        parts = pl.pallas_call(
            coulomb_kernel,
            out_shape=jax.ShapeDtypeStruct((NZ, rows, rows), F32),
            in_specs=[vmem] * 16,
            out_specs=vmem,
            compiler_params=params,
        )(own, xlf, bof0, bof1, xh0, xh1, *near, *far)

    with jax.named_scope("ring"):
        up = shift(parts[4, :hr].astype(BF), "z", 1)
        down = shift(parts[4, hr:].astype(BF), "z", -1)
        up = jnp.concatenate([up.astype(F32) + parts[3, :hr], parts[3, hr:]])
        down = jnp.concatenate([parts[5, :hr], down.astype(F32) + parts[5, hr:]])
        for k in (2, 1, 0):
            up, down = shift(up.astype(BF), "z", 1), shift(down.astype(BF), "z", -1)
            if k:
                up, down = up.astype(F32) + parts[k], down.astype(F32) + parts[NZ - k]

    with jax.named_scope("combined"):
        comb = pl.pallas_call(
            combined_kernel,
            out_shape=jax.ShapeDtypeStruct((NXL, hr, rows), BF),
            in_specs=[smem] + [vmem] * 5,
            out_specs=vmem,
            scratch_shapes=[pltpu.VMEM((NXL, hr, rows), F32)],
            compiler_params=params,
        )(occ_energy, virt_energy[:, None], virt_energy[None, :], parts[0], up, down)
        up1, down1 = shift(comb, "z", 1), shift(comb, "z", -1)
        up2, down2 = shift(up1, "z", 1), shift(down1, "z", -1)
        up3, down3 = shift(up2, "z", 1), shift(down2, "z", -1)
        up4, down4 = shift(up3[:, :hr // 2], "z", 1), shift(down3[:, hr // 2:], "z", -1)
        combs = [comb, up1, down1, up2, down2, up3, down3, up4, down4]

    with jax.named_scope("gamma"):
        piece = hr // NZ

        def gamma_of(group, types):
            return pl.pallas_call(
                functools.partial(gamma_kernel, group=group),
                out_shape=[jax.ShapeDtypeStruct((NZ, piece, 2 * aux), t) for t in types],
                in_specs=[vmem] * 19,
                out_specs=[vmem] * 2,
                scratch_shapes=[pltpu.VMEM((NZ, NXL, hr, rows), BF)],
                compiler_params=params,
            )(*combs, *near, *far)

        to_xh, to_both = gamma_of(1, (BF, F32))
        part = NZ // 2
        via_both, via_xl = flip_x(to_xh[:part], 3), flip_x(to_xh[part:], 1)
        mine, to_xl = gamma_of(0, (F32, F32))
        to_both = jnp.concatenate([to_both[:part], to_both[part:] + via_xl.astype(F32)]).astype(BF)
        to_xl = jnp.concatenate([to_xl[:part] + via_both.astype(F32), to_xl[part:]]).astype(BF)
        from_both, from_xl = flip_x(to_both, 3), flip_x(to_xl, 1)
        total = (mine + from_xl.astype(F32) + from_both.astype(F32)).astype(BF)

    with jax.named_scope("spread"):
        got = [total[0]] + [shift(total[k], "z", k) for k in range(1, NZ)]
        out = pl.pallas_call(
            assemble_kernel,
            out_shape=jax.ShapeDtypeStruct((piece, NZ * 2 * aux), BF),
            in_specs=[vmem] * NZ,
            out_specs=vmem,
            compiler_params=pltpu.CompilerParams(vmem_limit_bytes=16 << 20),
        )(*got)
    return out.reshape(occ_g, piece // occ_g, NZ * 2 * aux)


def solution(mesh):
    split = Mesh(mesh.devices.reshape(NY, NXH, NC, NZ, NXL), ("y", "xh", "core", "z", "xl"))
    placed = (P(GRP, None, SH), P(GRP, None, SH), P(), P())
    return jax.shard_map(on_device, mesh=split, in_specs=placed, out_specs=P(GRP, SH, None), check_vma=False)
```

```python
import functools

import jax
import jax.numpy as jnp
from jax import lax
from jax.experimental import pallas as pl
from jax.experimental.pallas import tpu as pltpu
from jax.sharding import Mesh, PartitionSpec as P

BLK = 128
NY, NXH, NC, NZ, NXL = 4, 2, 2, 8, 2
GRP = ("y", "xh", "core")
SH = ("z", "xl")
X = ("xh", "xl")
BF = jnp.bfloat16
F32 = jnp.float32


def flip_x(value, bits):
    return lax.ppermute(value, X, [(i, i ^ bits) for i in range(NXH * NXL)])


def shift(value, axis, steps):
    count = lax.axis_size(axis)
    return lax.ppermute(value, axis, [(i, (i + steps) % count) for i in range(count)])


def flip_core(value):
    return lax.ppermute(value, "core", [(0, 1), (1, 0)])


def dot_t(a, b):
    return lax.dot_general(a, b, (((1,), (1,)), ((), ())), preferred_element_type=F32)


def coulomb_kernel(own, xlf, bof, xh, *refs):
    near, far, (out, send_up, send_down, stack, left) = refs[0:4], refs[4:8], refs[8:13]
    z, xl, c = lax.axis_index("z"), lax.axis_index("xl"), lax.axis_index("core")
    rows, half = own.shape

    def lay(mine, flipped, at):
        here, there = slice(at * half, (at + 1) * half), slice((1 - at) * half, (2 - at) * half)
        left[0:rows, here] = mine[...]
        left[0:rows, there] = flipped[...]
        left[rows:, here] = xh[...]
        left[rows:, there] = bof[...]

    @pl.when(xl == c)
    def _():
        lay(own, far[0], 0)

    @pl.when(xl != c)
    def _():
        lay(own, xlf, 1)

    for d in range(NY):
        for k, pieces in enumerate((near, far)):
            stack[d * rows:(d + 1) * rows, k * half:(k + 1) * half] = pieces[d][...]
    for pair in range(NY // 2):
        got = dot_t(left[...], stack[pair * 2 * rows:(pair + 1) * 2 * rows, :])
        for e in range(2):
            for dd in range(2):
                at = lax.rem(e * NY + pair * 2 + dd + NZ - z, NZ)
                out[at] = got[e * rows:(e + 1) * rows, dd * rows:(dd + 1) * rows]
    send_up[...] = out[NZ // 2, 0:rows // 2, :].astype(BF)
    send_down[...] = out[NZ // 2, rows // 2:rows, :].astype(BF)


def combined_kernel(occ_ref, v_col, v_row, mine, up, down, out, scr):
    y, xh, c, z, xl = (lax.axis_index(n) for n in ("y", "xh", "core", "z", "xl"))
    virt = v_row.shape[1]
    count = mine.shape[0] // virt
    e, d = z // NY, lax.rem(z, NY)
    row_occ = ((y * NXH + lax.rem(xh + e, NXH)) * NC + c) * count
    col_occ = ((lax.rem(y + NY - d, NY) * NXH + xh) * NC + xl) * count
    for i in range(count):
        for j in range(count):
            tile = (pl.ds(i * virt, virt), pl.ds(j * virt, virt))
            total = mine[tile] + up[tile].astype(F32) + down[tile].astype(F32)
            row, col = v_col[...] - occ_ref[row_occ + i], v_row[...] - occ_ref[col_occ + j]
            amp = (total / (row + col)).astype(BF).astype(F32)
            comb = 2.0 * amp - amp.T
            for zp in range(NZ):
                for h in range(NXL):
                    at = (zp * NXL + h) * 8
                    scr[h, (zp * count + i) * 8:(zp * count + i + 1) * 8, j * virt:(j + 1) * virt] = comb[at:at + 8]
    for h in range(NXL):
        out[h] = scr[h].astype(BF)


def gamma_kernel(*refs, group):
    combs, stack, outs, (left, scr) = refs[0:9], refs[9], refs[10:-2], refs[-2:]
    half, rows = combs[0].shape[1:]
    z, xl = lax.axis_index("z"), lax.axis_index("xl")
    part = combs[7].shape[1]
    places = [(ref, step, 0) for ref, step in zip(combs[:7], (0, 1, -1, 2, -2, 3, -3))]
    for ref, step, row0 in places + [(combs[7], 4, 0), (combs[8], 4, part)]:
        source = lax.rem(z + NZ - step, NZ)

        @pl.when(source // NY == group)
        def _(ref=ref, source=source, row0=row0):
            cols = pl.ds(pl.multiple_of(lax.rem(source, NY) * rows, 128), rows)
            for fl in range(2):
                at = fl * half + row0
                left[at:at + ref.shape[1], cols] = ref[lax.rem(xl + fl, 2)]

    width = stack.shape[1] // 2
    piece = half // NZ
    for k in range(2):
        cols = slice(k * width, (k + 1) * width)
        acc = jnp.dot(left[...], stack[:, cols], preferred_element_type=F32)
        for zp in range(NZ):
            at = lax.rem(zp + NZ - z, NZ)
            scr[0, at, :, cols] = acc[zp * piece:(zp + 1) * piece]
            scr[1, at, :, cols] = acc[half + zp * piece:half + (zp + 1) * piece]
    n = NZ // 2
    for fl in range(2):
        for p in range(2):
            outs[2 * fl + p][...] = scr[fl, p * n:(p + 1) * n].astype(outs[2 * fl + p].dtype)


def assemble_kernel(*refs):
    out = refs[-1]
    z, core = lax.axis_index("z"), lax.axis_index("core")
    half = refs[0].shape[1] // 2
    for k in range(NZ):
        source = lax.rem(z + NZ - k, NZ)
        for part in range(2):
            start = pl.multiple_of(source * 2 * half + lax.rem(core + part, 2) * half, 128)
            out[:, pl.ds(start, half)] = refs[k][:, part * half:(part + 1) * half]


def on_device(factors, screen, occ_energy, virt_energy):
    occ_g, virt, aux = factors.shape
    rows = occ_g * virt
    hr = rows // 2
    wide_mask = jnp.repeat(jnp.repeat(screen, BLK, axis=1), BLK, axis=2)
    own = (factors * wide_mask.astype(BF)).reshape(rows, aux)

    with jax.named_scope("gather"):
        j0 = lax.ppermute(own, ("core", "xl"), [(0, 0), (1, 2), (2, 1), (3, 3)])
        bof = flip_x(own, 3)
        xh = flip_x(own, 2)
        f0 = flip_core(j0)
        j1, j2, j3 = (shift(j0, "y", d) for d in (1, 2, 3))
        own_b, f0, bof, xh = lax.optimization_barrier((own, f0, bof, xh))
        xlf = lax.ppermute(own_b, ("core", "xl"), [(0, 1), (3, 2)])
        j1, j3, xlf = lax.optimization_barrier((j1, j3, xlf))
        near = [j0, j1, j2, j3]
        far = [f0] + [flip_core(p) for p in near[1:]]

    vmem = pl.BlockSpec(memory_space=pltpu.VMEM)
    smem = pl.BlockSpec(memory_space=pltpu.SMEM)
    params = pltpu.CompilerParams(vmem_limit_bytes=48 << 20)

    with jax.named_scope("coulomb"):
        parts, up, down, stack = pl.pallas_call(
            coulomb_kernel,
            out_shape=[
                jax.ShapeDtypeStruct((NZ, rows, rows), F32),
                jax.ShapeDtypeStruct((hr, rows), BF),
                jax.ShapeDtypeStruct((hr, rows), BF),
                jax.ShapeDtypeStruct((NY * rows, 2 * aux), BF),
            ],
            in_specs=[vmem] * 12,
            out_specs=[vmem] * 4,
            scratch_shapes=[pltpu.VMEM((2 * rows, 2 * aux), BF)],
            compiler_params=params,
        )(own, xlf, bof, xh, *near, *far)

    with jax.named_scope("ring"):
        up, down = shift(up, "z", 1), shift(down, "z", -1)
        up = jnp.concatenate([up.astype(F32) + parts[3, :hr], parts[3, hr:]])
        down = jnp.concatenate([parts[5, :hr], down.astype(F32) + parts[5, hr:]])
        for k in (2, 1, 0):
            up, down = shift(up.astype(BF), "z", 1), shift(down.astype(BF), "z", -1)
            if k:
                up, down = up.astype(F32) + parts[k], down.astype(F32) + parts[NZ - k]

    with jax.named_scope("combined"):
        comb = pl.pallas_call(
            combined_kernel,
            out_shape=jax.ShapeDtypeStruct((NXL, hr, rows), BF),
            in_specs=[smem] + [vmem] * 5,
            out_specs=vmem,
            scratch_shapes=[pltpu.VMEM((NXL, hr, rows), F32)],
            compiler_params=params,
        )(occ_energy, virt_energy[:, None], virt_energy[None, :], parts[0], up, down)
        up1, down1 = shift(comb, "z", 1), shift(comb, "z", -1)
        up2, down2 = shift(up1, "z", 1), shift(down1, "z", -1)
        up3, down3 = shift(up2, "z", 1), shift(down2, "z", -1)
        up4, down4 = shift(up3[:, :hr // 2], "z", 1), shift(down3[:, hr // 2:], "z", -1)
        combs = [comb, up1, down1, up2, down2, up3, down3, up4, down4]

    with jax.named_scope("gamma"):
        piece = hr // NZ

        def gamma_of(group, types):
            return pl.pallas_call(
                functools.partial(gamma_kernel, group=group),
                out_shape=[jax.ShapeDtypeStruct((NZ // 2, piece, 2 * aux), t) for t in types],
                in_specs=[vmem] * 10,
                out_specs=[vmem] * 4,
                scratch_shapes=[
                    pltpu.VMEM((2 * hr, NY * rows), BF),
                    pltpu.VMEM((2, NZ, piece, 2 * aux), F32),
                ],
                compiler_params=params,
            )(*combs, stack)

        to_xh0, to_xh1, to_both0, to_both1 = gamma_of(1, (BF, BF, F32, F32))
        via_both, via_xl = flip_x(to_xh0, 3), flip_x(to_xh1, 1)
        mine0, mine1, to_xl0, to_xl1 = gamma_of(0, (F32, F32, F32, F32))
        to_both = jnp.concatenate([to_both0, to_both1 + via_xl.astype(F32)]).astype(BF)
        to_xl = jnp.concatenate([to_xl0 + via_both.astype(F32), to_xl1]).astype(BF)
        mine = jnp.concatenate([mine0, mine1])
        from_both, from_xl = flip_x(to_both, 3), flip_x(to_xl, 1)
        total = (mine + from_xl.astype(F32) + from_both.astype(F32)).astype(BF)

    with jax.named_scope("spread"):
        got = [total[0]] + [shift(total[k], "z", k) for k in range(1, NZ)]
        out = pl.pallas_call(
            assemble_kernel,
            out_shape=jax.ShapeDtypeStruct((piece, NZ * 2 * aux), BF),
            in_specs=[vmem] * NZ,
            out_specs=vmem,
            compiler_params=pltpu.CompilerParams(vmem_limit_bytes=16 << 20),
        )(*got)
    return out.reshape(occ_g, piece // occ_g, NZ * 2 * aux)


def solution(mesh):
    split = Mesh(mesh.devices.reshape(NY, NXH, NC, NZ, NXL), ("y", "xh", "core", "z", "xl"))
    placed = (P(GRP, None, SH), P(GRP, None, SH), P(), P())
    return jax.shard_map(on_device, mesh=split, in_specs=placed, out_specs=P(GRP, SH, None), check_vma=False)
```

```python
import functools

import jax
import jax.numpy as jnp
from jax import lax
from jax.experimental import pallas as pl
from jax.experimental.pallas import tpu as pltpu
from jax.sharding import Mesh, PartitionSpec as P

BLK = 128
NY, NXH, NC, NZ, NXL = 4, 2, 2, 8, 2
GRP = ("y", "xh", "core")
SH = ("z", "xl")
X = ("xh", "xl")
BF = jnp.bfloat16
F32 = jnp.float32


def flip_x(value, bits):
    return lax.ppermute(value, X, [(i, i ^ bits) for i in range(NXH * NXL)])


def shift(value, axis, steps):
    count = lax.axis_size(axis)
    return lax.ppermute(value, axis, [(i, (i + steps) % count) for i in range(count)])


def flip_core(value):
    return lax.ppermute(value, "core", [(0, 1), (1, 0)])


def dot_t(a, b):
    return lax.dot_general(a, b, (((1,), (1,)), ((), ())), preferred_element_type=F32)


def coulomb_kernel(own, xlf, bof, xh0, xh1, *refs):
    near, far, (out, mine, send_up, send_down, keep_up, keep_down, stack, left) = refs[0:5], refs[5:10], refs[10:18]
    z, xl, c = lax.axis_index("z"), lax.axis_index("xl"), lax.axis_index("core")
    rows, half = own.shape

    def lay(mine, flipped, at):
        here, there = slice(at * half, (at + 1) * half), slice((1 - at) * half, (2 - at) * half)
        left[0:rows, here] = mine[...]
        left[0:rows, there] = flipped[...]
        left[rows:rows + rows // 2, here] = xh0[...]
        left[rows + rows // 2:, here] = xh1[...]
        left[rows:, there] = bof[...]

    @pl.when(xl == c)
    def _():
        lay(own, far[0], 0)

    @pl.when(xl != c)
    def _():
        lay(own, xlf, 1)

    for k, pieces in enumerate((near, far)):
        at = 0
        for piece in pieces:
            stack[at:at + piece.shape[0], k * half:(k + 1) * half] = piece[...]
            at += piece.shape[0]
    for pair in range(NY // 2):
        got = dot_t(left[...], stack[pair * 2 * rows:(pair + 1) * 2 * rows, :])
        for e in range(2):
            for dd in range(2):
                at = lax.rem(e * NY + pair * 2 + dd + NZ - z, NZ)
                out[at] = got[e * rows:(e + 1) * rows, dd * rows:(dd + 1) * rows]
    low, high = slice(0, rows // 2), slice(rows // 2, rows)
    mine[...] = out[0]
    send_up[...], send_down[...] = out[NZ // 2, low, :].astype(BF), out[NZ // 2, high, :].astype(BF)
    keep_up[...], keep_down[...] = out[NZ // 2 - 1, high, :].astype(BF), out[NZ // 2 + 1, low, :].astype(BF)


def combined_kernel(occ_ref, v_col, v_row, mine, up, down, out, scr):
    y, xh, c, z, xl = (lax.axis_index(n) for n in ("y", "xh", "core", "z", "xl"))
    virt = v_row.shape[1]
    count = mine.shape[0] // virt
    e, d = z // NY, lax.rem(z, NY)
    row_occ = ((y * NXH + lax.rem(xh + e, NXH)) * NC + c) * count
    col_occ = ((lax.rem(y + NY - d, NY) * NXH + xh) * NC + xl) * count
    for i in range(count):
        for j in range(count):
            tile = (pl.ds(i * virt, virt), pl.ds(j * virt, virt))
            total = mine[tile] + up[tile].astype(F32) + down[tile].astype(F32)
            row, col = v_col[...] - occ_ref[row_occ + i], v_row[...] - occ_ref[col_occ + j]
            amp = (total / (row + col)).astype(BF).astype(F32)
            comb = 2.0 * amp - amp.T
            for zp in range(NZ):
                for h in range(NXL):
                    at = (zp * NXL + h) * 8
                    scr[h, (zp * count + i) * 8:(zp * count + i + 1) * 8, j * virt:(j + 1) * virt] = comb[at:at + 8]
    for h in range(NXL):
        out[h] = scr[h].astype(BF)


def gamma_kernel(*refs, group):
    combs, stack, outs, (left, scr) = refs[0:9], refs[9], refs[10:-2], refs[-2:]
    half, rows = combs[0].shape[1:]
    z, xl = lax.axis_index("z"), lax.axis_index("xl")
    part = combs[7].shape[1]
    places = [(ref, step, 0) for ref, step in zip(combs[:7], (0, 1, -1, 2, -2, 3, -3))]
    for ref, step, row0 in places + [(combs[7], 4, 0), (combs[8], 4, part)]:
        source = lax.rem(z + NZ - step, NZ)

        @pl.when(source // NY == group)
        def _(ref=ref, source=source, row0=row0):
            cols = pl.ds(pl.multiple_of(lax.rem(source, NY) * rows, 128), rows)
            for fl in range(2):
                at = fl * half + row0
                left[at:at + ref.shape[1], cols] = ref[lax.rem(xl + fl, 2)]

    width = stack.shape[1] // 2
    piece = half // NZ
    for k in range(2):
        cols = slice(k * width, (k + 1) * width)
        acc = jnp.dot(left[...], stack[:, cols], preferred_element_type=F32)
        for zp in range(NZ):
            at = lax.rem(zp + NZ - z, NZ)
            scr[0, at, :, cols] = acc[zp * piece:(zp + 1) * piece]
            scr[1, at, :, cols] = acc[half + zp * piece:half + (zp + 1) * piece]
    n = NZ // 2
    for fl in range(2):
        for p in range(2):
            outs[2 * fl + p][...] = scr[fl, p * n:(p + 1) * n].astype(outs[2 * fl + p].dtype)


def assemble_kernel(*refs):
    out = refs[-1]
    z, core = lax.axis_index("z"), lax.axis_index("core")
    half = refs[0].shape[1] // 2
    for k in range(NZ):
        source = lax.rem(z + NZ - k, NZ)
        for part in range(2):
            start = pl.multiple_of(source * 2 * half + lax.rem(core + part, 2) * half, 128)
            out[:, pl.ds(start, half)] = refs[k][:, part * half:(part + 1) * half]


def on_device(factors, screen, occ_energy, virt_energy):
    occ_g, virt, aux = factors.shape
    rows = occ_g * virt
    hr = rows // 2
    wide_mask = jnp.repeat(jnp.repeat(screen, BLK, axis=1), BLK, axis=2)
    own = (factors * wide_mask.astype(BF)).reshape(rows, aux)

    with jax.named_scope("gather"):
        j0 = lax.ppermute(own, ("core", "xl"), [(0, 0), (1, 2), (2, 1), (3, 3)])
        bof = flip_x(own, 3)
        xlf = lax.ppermute(own, ("core", "xl"), [(0, 1), (3, 2)])
        j1, j3 = shift(j0, "y", 1), shift(j0, "y", -1)
        f0 = flip_core(j0)
        bof, xlf, f0 = lax.optimization_barrier((bof, xlf, f0))
        same = lax.axis_index("xl") == lax.axis_index("core")
        xh0 = flip_x(jnp.where(same, f0[:hr], xlf[:hr]), 3)
        xh1 = flip_x(bof[hr:], 1)
        j1, j3, xh0, xh1 = lax.optimization_barrier((j1, j3, xh0, xh1))
        j2a, j2b = shift(j1[:hr], "y", 1), shift(j3[hr:], "y", -1)
        near = [j0, j1, j2a, j2b, j3]
        far = [f0] + [flip_core(p) for p in near[1:]]

    vmem = pl.BlockSpec(memory_space=pltpu.VMEM)
    smem = pl.BlockSpec(memory_space=pltpu.SMEM)
    params = pltpu.CompilerParams(vmem_limit_bytes=48 << 20)

    with jax.named_scope("coulomb"):
        parts, mine, up, down, keep_up, keep_down, stack = pl.pallas_call(
            coulomb_kernel,
            out_shape=[
                jax.ShapeDtypeStruct((NZ, rows, rows), F32),
                jax.ShapeDtypeStruct((rows, rows), F32),
                jax.ShapeDtypeStruct((hr, rows), BF),
                jax.ShapeDtypeStruct((hr, rows), BF),
                jax.ShapeDtypeStruct((hr, rows), BF),
                jax.ShapeDtypeStruct((hr, rows), BF),
                jax.ShapeDtypeStruct((NY * rows, 2 * aux), BF),
            ],
            in_specs=[vmem] * 15,
            out_specs=[vmem] * 7,
            scratch_shapes=[pltpu.VMEM((2 * rows, 2 * aux), BF)],
            compiler_params=params,
        )(own, xlf, bof, xh0, xh1, *near, *far)

    with jax.named_scope("ring"):
        up, down = shift(up, "z", 1), shift(down, "z", -1)
        up = jnp.concatenate([(up.astype(F32) + parts[3, :hr]).astype(BF), keep_up])
        down = jnp.concatenate([keep_down, (down.astype(F32) + parts[5, hr:]).astype(BF)])
        for k in (2, 1, 0):
            up, down = shift(up, "z", 1), shift(down, "z", -1)
            if k:
                up = (up.astype(F32) + parts[k]).astype(BF)
                down = (down.astype(F32) + parts[NZ - k]).astype(BF)

    with jax.named_scope("combined"):
        comb = pl.pallas_call(
            combined_kernel,
            out_shape=jax.ShapeDtypeStruct((NXL, hr, rows), BF),
            in_specs=[smem] + [vmem] * 5,
            out_specs=vmem,
            scratch_shapes=[pltpu.VMEM((NXL, hr, rows), F32)],
            compiler_params=params,
        )(occ_energy, virt_energy[:, None], virt_energy[None, :], mine, up, down)
        up1, down1 = shift(comb, "z", 1), shift(comb, "z", -1)
        up2, down2 = shift(up1, "z", 1), shift(down1, "z", -1)
        up3, down3 = shift(up2, "z", 1), shift(down2, "z", -1)
        up4, down4 = shift(up3[:, :hr // 2], "z", 1), shift(down3[:, hr // 2:], "z", -1)
        combs = [comb, up1, down1, up2, down2, up3, down3, up4, down4]

    with jax.named_scope("gamma"):
        piece = hr // NZ

        def gamma_of(group, types):
            return pl.pallas_call(
                functools.partial(gamma_kernel, group=group),
                out_shape=[jax.ShapeDtypeStruct((NZ // 2, piece, 2 * aux), t) for t in types],
                in_specs=[vmem] * 10,
                out_specs=[vmem] * 4,
                scratch_shapes=[
                    pltpu.VMEM((2 * hr, NY * rows), BF),
                    pltpu.VMEM((2, NZ, piece, 2 * aux), F32),
                ],
                compiler_params=params,
            )(*combs, stack)

        to_xh0, to_xh1, to_both0, to_both1 = gamma_of(1, (BF, BF, F32, F32))
        via_both, via_xl = flip_x(to_xh0, 3), flip_x(to_xh1, 1)
        mine0, mine1, to_xl0, to_xl1 = gamma_of(0, (F32, F32, F32, F32))
        to_both = jnp.concatenate([to_both0, to_both1 + via_xl.astype(F32)]).astype(BF)
        to_xl = jnp.concatenate([to_xl0 + via_both.astype(F32), to_xl1]).astype(BF)
        kept = jnp.concatenate([mine0, mine1])
        from_both, from_xl = flip_x(to_both, 3), flip_x(to_xl, 1)
        total = (kept + from_xl.astype(F32) + from_both.astype(F32)).astype(BF)

    with jax.named_scope("spread"):
        got = [total[0]] + [shift(total[k], "z", k) for k in range(1, NZ)]
        out = pl.pallas_call(
            assemble_kernel,
            out_shape=jax.ShapeDtypeStruct((piece, NZ * 2 * aux), BF),
            in_specs=[vmem] * NZ,
            out_specs=vmem,
            compiler_params=pltpu.CompilerParams(vmem_limit_bytes=16 << 20),
        )(*got)
    return out.reshape(occ_g, piece // occ_g, NZ * 2 * aux)


def solution(mesh):
    split = Mesh(mesh.devices.reshape(NY, NXH, NC, NZ, NXL), ("y", "xh", "core", "z", "xl"))
    placed = (P(GRP, None, SH), P(GRP, None, SH), P(), P())
    return jax.shard_map(on_device, mesh=split, in_specs=placed, out_specs=P(GRP, SH, None), check_vma=False)
```

```python
import functools

import jax
import jax.numpy as jnp
from jax import lax
from jax.experimental import pallas as pl
from jax.experimental.pallas import tpu as pltpu
from jax.sharding import Mesh, PartitionSpec as P

BLK = 128
NY, NXH, NC, NZ, NXL = 4, 2, 2, 8, 2
GRP = ("y", "xh", "core")
SH = ("z", "xl")
X = ("xh", "xl")
BF = jnp.bfloat16
COLUMNS = (0, 1, 3, 2)
F32 = jnp.float32


def flip_x(value, bits):
    return lax.ppermute(value, X, [(i, i ^ bits) for i in range(NXH * NXL)])


def shift(value, axis, steps):
    count = lax.axis_size(axis)
    return lax.ppermute(value, axis, [(i, (i + steps) % count) for i in range(count)])


def flip_core(value):
    return lax.ppermute(value, "core", [(0, 1), (1, 0)])


def dot_t(a, b):
    return lax.dot_general(a, b, (((1,), (1,)), ((), ())), preferred_element_type=F32)


def coulomb_kernel(own, xlf, bof, xh, *refs):
    near, far, (p0, p1, p2, p3, p5, p6, p7), refs = refs[0:3], refs[3:6], refs[6:13], refs[13:]
    send_up, send_down, keep_up, keep_down, stack_out, out, stack, left, sem = refs
    z, xl, c = lax.axis_index("z"), lax.axis_index("xl"), lax.axis_index("core")
    rows, half = own.shape

    for k, pieces in enumerate((near, far)):
        at = 0
        for piece in pieces:
            stack[at:at + piece.shape[0], k * half:(k + 1) * half] = piece[...]
            at += piece.shape[0]
    copy = pltpu.make_async_copy(stack, stack_out, sem)
    copy.start()

    def lay(mine, flipped, at):
        here, there = slice(at * half, (at + 1) * half), slice((1 - at) * half, (2 - at) * half)
        left[0:rows, here] = mine[...]
        left[0:rows, there] = flipped[...]
        left[rows:, here] = xh[...]
        left[rows:, there] = bof[...]

    @pl.when(xl == c)
    def _():
        lay(own, far[0], 0)

    @pl.when(xl != c)
    def _():
        lay(own, xlf, 1)

    for pair in range(NY // 2):
        got = dot_t(left[...], stack[pair * 2 * rows:(pair + 1) * 2 * rows, :])
        for e in range(2):
            for dd in range(2):
                at = lax.rem(e * NY + pair * 2 + dd + NZ - z, NZ)
                out[at] = got[e * rows:(e + 1) * rows, dd * rows:(dd + 1) * rows]
    low, high = slice(0, rows // 2), slice(rows // 2, rows)
    for k, ref in ((0, p0), (1, p1), (2, p2), (6, p6), (7, p7)):
        ref[...] = out[k]
    p3[...], p5[...] = out[3, low, :], out[5, high, :]
    send_up[...], send_down[...] = out[4, low, :].astype(BF), out[4, high, :].astype(BF)
    keep_up[...], keep_down[...] = out[3, high, :].astype(BF), out[5, low, :].astype(BF)
    copy.wait()


def combined_kernel(occ_ref, v_col, v_row, mine, up, down, out, scr):
    y, xh, c, z, xl = (lax.axis_index(n) for n in ("y", "xh", "core", "z", "xl"))
    virt = v_row.shape[1]
    count = mine.shape[0] // virt
    e, d = z // NY, lax.rem(z, NY)
    row_occ = ((y * NXH + lax.rem(xh + e, NXH)) * NC + c) * count
    back = jnp.where(d < 2, d, NY + 1 - d)
    col_occ = ((lax.rem(y + NY - back, NY) * NXH + xh) * NC + xl) * count
    for i in range(count):
        for j in range(count):
            tile = (pl.ds(i * virt, virt), pl.ds(j * virt, virt))
            total = mine[tile] + up[tile].astype(F32) + down[tile].astype(F32)
            row, col = v_col[...] - occ_ref[row_occ + i], v_row[...] - occ_ref[col_occ + j]
            amp = (total / (row + col)).astype(BF).astype(F32)
            comb = 2.0 * amp - amp.T
            for zp in range(NZ):
                for h in range(NXL):
                    at = (zp * NXL + h) * 8
                    scr[h, (zp * count + i) * 8:(zp * count + i + 1) * 8, j * virt:(j + 1) * virt] = comb[at:at + 8]
    for h in range(NXL):
        out[h] = scr[h].astype(BF)


def gamma_kernel(*refs, group):
    combs, stack, outs, (left, scr) = refs[0:9], refs[9], refs[10:-2], refs[-2:]
    half, rows = combs[0].shape[1:]
    z, xl = lax.axis_index("z"), lax.axis_index("xl")
    part = combs[7].shape[1]
    places = [(ref, step, 0) for ref, step in zip(combs[:7], (0, 1, -1, 2, -2, 3, -3))]
    for ref, step, row0 in places + [(combs[7], 4, 0), (combs[8], 4, part)]:
        source = lax.rem(z + NZ - step, NZ)

        @pl.when(source // NY == group)
        def _(ref=ref, source=source, row0=row0):
            cols = pl.ds(pl.multiple_of(lax.rem(source, NY) * rows, 128), rows)
            for fl in range(2):
                at = fl * half + row0
                left[at:at + ref.shape[1], cols] = ref[lax.rem(xl + fl, 2)]

    width = stack.shape[1] // 2
    piece = half // NZ
    for k in range(2):
        cols = slice(k * width, (k + 1) * width)
        acc = jnp.dot(left[...], stack[:, cols], preferred_element_type=F32)
        for zp in range(NZ):
            at = lax.rem(zp + NZ - z, NZ)
            scr[0, at, :, cols] = acc[zp * piece:(zp + 1) * piece]
            scr[1, at, :, cols] = acc[half + zp * piece:half + (zp + 1) * piece]
    n = NZ // 2
    for fl in range(2):
        for p in range(2):
            outs[2 * fl + p][...] = scr[fl, p * n:(p + 1) * n].astype(outs[2 * fl + p].dtype)


def assemble_kernel(*refs):
    out = refs[-1]
    z, core = lax.axis_index("z"), lax.axis_index("core")
    half = refs[0].shape[1] // 2
    for k in range(NZ):
        source = lax.rem(z + NZ - k, NZ)
        for part in range(2):
            start = pl.multiple_of(source * 2 * half + lax.rem(core + part, 2) * half, 128)
            out[:, pl.ds(start, half)] = refs[k][:, part * half:(part + 1) * half]


def on_device(factors, screen, occ_energy, virt_energy):
    occ_g, virt, aux = factors.shape
    rows = occ_g * virt
    hr = rows // 2
    wide_mask = jnp.repeat(jnp.repeat(screen, BLK, axis=1), BLK, axis=2)
    own = (factors * wide_mask.astype(BF)).reshape(rows, aux)

    with jax.named_scope("gather"):
        j0 = lax.ppermute(own, ("core", "xl"), [(0, 0), (1, 2), (2, 1), (3, 3)])
        bof = flip_x(own, 3)
        xlf = lax.ppermute(own, ("core", "xl"), [(0, 1), (3, 2)])
        j1, j3 = shift(j0, "y", 1), shift(j0, "y", -1)
        f0 = flip_core(j0)
        own_b, f0, xlf = lax.optimization_barrier((own, f0, xlf))
        xh = flip_x(own_b, 2)
        j1, j3, bof = lax.optimization_barrier((j1, j3, bof))
        j2a, j2b = shift(j1[:hr], "y", 1), shift(j3[hr:], "y", -1)
        j2a, j2b, xh = lax.optimization_barrier((j2a, j2b, xh))
        outer = jnp.concatenate([j1, j3])
        outer_far = flip_core(outer)
        inner = jnp.concatenate([j2a, j2b])
        inner_far = flip_core(inner)
        near, far = [j0, outer, inner], [f0, outer_far, inner_far]

    vmem = pl.BlockSpec(memory_space=pltpu.VMEM)
    smem = pl.BlockSpec(memory_space=pltpu.SMEM)
    params = pltpu.CompilerParams(vmem_limit_bytes=48 << 20)

    with jax.named_scope("coulomb"):
        whole, part = jax.ShapeDtypeStruct((rows, rows), F32), jax.ShapeDtypeStruct((hr, rows), F32)
        sent = jax.ShapeDtypeStruct((hr, rows), BF)
        mine, p1, p2, p3, p5, p6, p7, up, down, keep_up, keep_down, stack = pl.pallas_call(
            coulomb_kernel,
            out_shape=[whole, whole, whole, part, part, whole, whole, sent, sent, sent, sent]
            + [jax.ShapeDtypeStruct((NY * rows, 2 * aux), BF)],
            in_specs=[vmem] * 10,
            out_specs=[vmem] * 11 + [pl.BlockSpec(memory_space=pl.ANY)],
            scratch_shapes=[
                pltpu.VMEM((NZ, rows, rows), F32),
                pltpu.VMEM((NY * rows, 2 * aux), BF),
                pltpu.VMEM((2 * rows, 2 * aux), BF),
                pltpu.SemaphoreType.DMA,
            ],
            compiler_params=params,
        )(own, xlf, bof, xh, *near, *far)

    with jax.named_scope("ring"):
        up, down = shift(up, "z", 1), shift(down, "z", -1)
        up = jnp.concatenate([(up.astype(F32) + p3).astype(BF), keep_up])
        down = jnp.concatenate([keep_down, (down.astype(F32) + p5).astype(BF)])
        for from_up, from_down in ((p2, p6), (p1, p7), (None, None)):
            up, down = shift(up, "z", 1), shift(down, "z", -1)
            if from_up is not None:
                up = (up.astype(F32) + from_up).astype(BF)
                down = (down.astype(F32) + from_down).astype(BF)

    with jax.named_scope("combined"):
        comb = pl.pallas_call(
            combined_kernel,
            out_shape=jax.ShapeDtypeStruct((NXL, hr, rows), BF),
            in_specs=[smem] + [vmem] * 5,
            out_specs=vmem,
            scratch_shapes=[pltpu.VMEM((NXL, hr, rows), F32)],
            compiler_params=params,
        )(occ_energy, virt_energy[:, None], virt_energy[None, :], mine, up, down)
        up1, down1 = shift(comb, "z", 1), shift(comb, "z", -1)
        up2, down2 = shift(up1, "z", 1), shift(down1, "z", -1)
        up3, down3 = shift(up2, "z", 1), shift(down2, "z", -1)
        up4, down4 = shift(up3[:, :hr // 2], "z", 1), shift(down3[:, hr // 2:], "z", -1)
        combs = [comb, up1, down1, up2, down2, up3, down3, up4, down4]

    with jax.named_scope("gamma"):
        piece = hr // NZ

        def gamma_of(group, types):
            return pl.pallas_call(
                functools.partial(gamma_kernel, group=group),
                out_shape=[jax.ShapeDtypeStruct((NZ // 2, piece, 2 * aux), t) for t in types],
                in_specs=[vmem] * 10,
                out_specs=[vmem] * 4,
                scratch_shapes=[
                    pltpu.VMEM((2 * hr, NY * rows), BF),
                    pltpu.VMEM((2, NZ, piece, 2 * aux), F32),
                ],
                compiler_params=params,
            )(*combs, stack)

        to_xh0, to_xh1, to_both0, to_both1 = gamma_of(1, (BF, BF, F32, F32))
        via_both, via_xl = flip_x(to_xh0, 3), flip_x(to_xh1, 1)
        mine0, mine1, to_xl0, to_xl1 = gamma_of(0, (F32, F32, F32, F32))
        to_both = jnp.concatenate([to_both0, to_both1 + via_xl.astype(F32)]).astype(BF)
        to_xl = jnp.concatenate([to_xl0 + via_both.astype(F32), to_xl1]).astype(BF)
        kept = jnp.concatenate([mine0, mine1])
        from_both, from_xl = flip_x(to_both, 3), flip_x(to_xl, 1)
        total = (kept + from_xl.astype(F32) + from_both.astype(F32)).astype(BF)

    with jax.named_scope("spread"):
        got = [total[0]] + [shift(total[k], "z", k) for k in range(1, NZ)]
        out = pl.pallas_call(
            assemble_kernel,
            out_shape=jax.ShapeDtypeStruct((piece, NZ * 2 * aux), BF),
            in_specs=[vmem] * NZ,
            out_specs=vmem,
            compiler_params=pltpu.CompilerParams(vmem_limit_bytes=16 << 20),
        )(*got)
    return out.reshape(occ_g, piece // occ_g, NZ * 2 * aux)


def solution(mesh):
    split = Mesh(mesh.devices.reshape(NY, NXH, NC, NZ, NXL), ("y", "xh", "core", "z", "xl"))
    placed = (P(GRP, None, SH), P(GRP, None, SH), P(), P())
    return jax.shard_map(on_device, mesh=split, in_specs=placed, out_specs=P(GRP, SH, None), check_vma=False)
```

```python
import functools

import jax
import jax.numpy as jnp
from jax import lax
from jax.experimental import pallas as pl
from jax.experimental.pallas import tpu as pltpu
from jax.sharding import Mesh, PartitionSpec as P

BLK = 128
NY, NXH, NC, NZ, NXL = 4, 2, 2, 8, 2
GRP = ("y", "xh", "core")
SH = ("z", "xl")
X = ("xh", "xl")
BF = jnp.bfloat16
COLUMNS = (0, 1, 3, 2)
F32 = jnp.float32


def flip_x(value, bits):
    return lax.ppermute(value, X, [(i, i ^ bits) for i in range(NXH * NXL)])


def shift(value, axis, steps):
    count = lax.axis_size(axis)
    return lax.ppermute(value, axis, [(i, (i + steps) % count) for i in range(count)])


def flip_core(value):
    return lax.ppermute(value, "core", [(0, 1), (1, 0)])


def dot_t(a, b):
    return lax.dot_general(a, b, (((1,), (1,)), ((), ())), preferred_element_type=F32)


def coulomb_kernel(own, xlf, bof, xh, *refs):
    near, far, (p0, p1, p2, p3, p5, p6, p7), refs = refs[0:3], refs[3:6], refs[6:13], refs[13:]
    send_up, send_down, keep_up, keep_down, stack_out, out, stack, left, sem = refs
    z, xl, c = lax.axis_index("z"), lax.axis_index("xl"), lax.axis_index("core")
    rows, half = own.shape

    for k, pieces in enumerate((near, far)):
        at = 0
        for piece in pieces:
            stack[at:at + piece.shape[0], k * half:(k + 1) * half] = piece[...]
            at += piece.shape[0]
    copy = pltpu.make_async_copy(stack, stack_out, sem)
    copy.start()

    def lay(mine, flipped, at):
        here, there = slice(at * half, (at + 1) * half), slice((1 - at) * half, (2 - at) * half)
        left[0:rows, here] = mine[...]
        left[0:rows, there] = flipped[...]
        left[rows:, here] = xh[...]
        left[rows:, there] = bof[...]

    @pl.when(xl == c)
    def _():
        lay(own, far[0], 0)

    @pl.when(xl != c)
    def _():
        lay(own, xlf, 1)

    for pair in range(NY // 2):
        got = dot_t(left[...], stack[pair * 2 * rows:(pair + 1) * 2 * rows, :])
        for e in range(2):
            for dd in range(2):
                at = lax.rem(e * NY + pair * 2 + dd + NZ - z, NZ)
                out[at] = got[e * rows:(e + 1) * rows, dd * rows:(dd + 1) * rows]
    low, high = slice(0, rows // 2), slice(rows // 2, rows)
    for k, ref in ((0, p0), (1, p1), (2, p2), (6, p6), (7, p7)):
        ref[...] = out[k]
    p3[...], p5[...] = out[3, low, :], out[5, high, :]
    send_up[...], send_down[...] = out[4, low, :].astype(BF), out[4, high, :].astype(BF)
    keep_up[...], keep_down[...] = out[3, high, :].astype(BF), out[5, low, :].astype(BF)
    copy.wait()


def combined_kernel(occ_ref, v_col, v_row, mine, up, down, out, scr):
    y, xh, c, z, xl = (lax.axis_index(n) for n in ("y", "xh", "core", "z", "xl"))
    virt = v_row.shape[1]
    count = mine.shape[0] // virt
    e, d = z // NY, lax.rem(z, NY)
    row_occ = ((y * NXH + lax.rem(xh + e, NXH)) * NC + c) * count
    back = jnp.where(d < 2, d, NY + 1 - d)
    col_occ = ((lax.rem(y + NY - back, NY) * NXH + xh) * NC + xl) * count
    for i in range(count):
        for j in range(count):
            tile = (pl.ds(i * virt, virt), pl.ds(j * virt, virt))
            total = mine[tile] + up[tile].astype(F32) + down[tile].astype(F32)
            row, col = v_col[...] - occ_ref[row_occ + i], v_row[...] - occ_ref[col_occ + j]
            amp = (total / (row + col)).astype(BF).astype(F32)
            comb = 2.0 * amp - amp.T
            for zp in range(NZ):
                for h in range(NXL):
                    at = (zp * NXL + h) * 8
                    scr[h, (zp * count + i) * 8:(zp * count + i + 1) * 8, j * virt:(j + 1) * virt] = comb[at:at + 8]
    for h in range(NXL):
        out[h] = scr[h].astype(BF)


def gamma_kernel(*refs, group):
    combs, stack, outs, (left, scr) = refs[0:9], refs[9], refs[10:-2], refs[-2:]
    half, rows = combs[0].shape[1:]
    z, xl = lax.axis_index("z"), lax.axis_index("xl")
    part = combs[7].shape[1]
    places = [(ref, step, 0) for ref, step in zip(combs[:7], (0, 1, -1, 2, -2, 3, -3))]
    for ref, step, row0 in places + [(combs[7], 4, 0), (combs[8], 4, part)]:
        source = lax.rem(z + NZ - step, NZ)

        @pl.when(source // NY == group)
        def _(ref=ref, source=source, row0=row0):
            cols = pl.ds(pl.multiple_of(lax.rem(source, NY) * rows, 128), rows)
            for fl in range(2):
                at = fl * half + row0
                left[at:at + ref.shape[1], cols] = ref[lax.rem(xl + fl, 2)]

    width = stack.shape[1] // 2
    piece = half // NZ
    for k in range(2):
        cols = slice(k * width, (k + 1) * width)
        acc = jnp.dot(left[...], stack[:, cols], preferred_element_type=F32)
        for zp in range(NZ):
            at = lax.rem(zp + NZ - z, NZ)
            scr[0, at, :, cols] = acc[zp * piece:(zp + 1) * piece]
            scr[1, at, :, cols] = acc[half + zp * piece:half + (zp + 1) * piece]
    n = NZ // 2
    for fl in range(2):
        for p in range(2):
            outs[2 * fl + p][...] = scr[fl, p * n:(p + 1) * n].astype(outs[2 * fl + p].dtype)


def assemble_kernel(*refs):
    out = refs[-1]
    z, core = lax.axis_index("z"), lax.axis_index("core")
    half = refs[0].shape[1] // 2
    for k in range(NZ):
        source = lax.rem(z + NZ - k, NZ)
        for part in range(2):
            start = pl.multiple_of(source * 2 * half + lax.rem(core + part, 2) * half, 128)
            out[:, pl.ds(start, half)] = refs[k][:, part * half:(part + 1) * half]


def on_device(factors, screen, occ_energy, virt_energy):
    occ_g, virt, aux = factors.shape
    rows = occ_g * virt
    hr = rows // 2
    wide_mask = jnp.repeat(jnp.repeat(screen, BLK, axis=1), BLK, axis=2)
    own = (factors * wide_mask.astype(BF)).reshape(rows, aux)

    with jax.named_scope("gather"):
        j0 = lax.ppermute(own, ("core", "xl"), [(0, 0), (1, 2), (2, 1), (3, 3)])
        bof = flip_x(own, 3)
        xlf = lax.ppermute(own, ("core", "xl"), [(0, 1), (3, 2)])
        j1, j3 = shift(j0, "y", 1), shift(j0, "y", -1)
        f0 = flip_core(j0)
        own_b, f0, xlf = lax.optimization_barrier((own, f0, xlf))
        xh = flip_x(own_b, 2)
        j1, j3, bof = lax.optimization_barrier((j1, j3, bof))
        j2a, j2b = shift(j1[:hr], "y", 1), shift(j3[hr:], "y", -1)
        j2a, j2b, xh = lax.optimization_barrier((j2a, j2b, xh))
        outer = jnp.concatenate([j1, j3])
        outer_far = flip_core(outer)
        inner = jnp.concatenate([j2a, j2b])
        inner_far = flip_core(inner)
        near, far = [j0, outer, inner], [f0, outer_far, inner_far]

    vmem = pl.BlockSpec(memory_space=pltpu.VMEM)
    smem = pl.BlockSpec(memory_space=pltpu.SMEM)
    params = pltpu.CompilerParams(vmem_limit_bytes=48 << 20)

    with jax.named_scope("coulomb"):
        whole, part = jax.ShapeDtypeStruct((rows, rows), F32), jax.ShapeDtypeStruct((hr, rows), F32)
        sent = jax.ShapeDtypeStruct((hr, rows), BF)
        mine, p1, p2, p3, p5, p6, p7, up, down, keep_up, keep_down, stack = pl.pallas_call(
            coulomb_kernel,
            out_shape=[whole, whole, whole, part, part, whole, whole, sent, sent, sent, sent]
            + [jax.ShapeDtypeStruct((NY * rows, 2 * aux), BF)],
            in_specs=[vmem] * 10,
            out_specs=[vmem] * 11 + [pl.BlockSpec(memory_space=pl.ANY)],
            scratch_shapes=[
                pltpu.VMEM((NZ, rows, rows), F32),
                pltpu.VMEM((NY * rows, 2 * aux), BF),
                pltpu.VMEM((2 * rows, 2 * aux), BF),
                pltpu.SemaphoreType.DMA,
            ],
            compiler_params=params,
        )(own, xlf, bof, xh, *near, *far)

    with jax.named_scope("ring"):
        up, down = shift(up, "z", 1), shift(down, "z", -1)
        up = jnp.concatenate([(up.astype(F32) + p3).astype(BF), keep_up])
        down = jnp.concatenate([keep_down, (down.astype(F32) + p5).astype(BF)])
        for from_up, from_down in ((p2, p6), (p1, p7), (None, None)):
            up, down = shift(up, "z", 1), shift(down, "z", -1)
            if from_up is not None:
                up = (up.astype(F32) + from_up).astype(BF)
                down = (down.astype(F32) + from_down).astype(BF)

    with jax.named_scope("combined"):
        comb = pl.pallas_call(
            combined_kernel,
            out_shape=jax.ShapeDtypeStruct((NXL, hr, rows), BF),
            in_specs=[smem] + [vmem] * 5,
            out_specs=vmem,
            scratch_shapes=[pltpu.VMEM((NXL, hr, rows), F32)],
            compiler_params=params,
        )(occ_energy, virt_energy[:, None], virt_energy[None, :], mine, up, down)
        up1, down1 = shift(comb, "z", 1), shift(comb, "z", -1)
        up2, down2 = shift(up1, "z", 1), shift(down1, "z", -1)
        up3, down3 = shift(up2, "z", 1), shift(down2, "z", -1)
        up4, down4 = shift(up3[:, :hr // 2], "z", 1), shift(down3[:, hr // 2:], "z", -1)
        combs = [comb, up1, down1, up2, down2, up3, down3, up4, down4]

    with jax.named_scope("gamma"):
        piece = hr // NZ

        def gamma_of(group, types):
            return pl.pallas_call(
                functools.partial(gamma_kernel, group=group),
                out_shape=[jax.ShapeDtypeStruct((NZ // 2, piece, 2 * aux), t) for t in types],
                in_specs=[vmem] * 10,
                out_specs=[vmem] * 4,
                scratch_shapes=[
                    pltpu.VMEM((2 * hr, NY * rows), BF),
                    pltpu.VMEM((2, NZ, piece, 2 * aux), F32),
                ],
                compiler_params=params,
            )(*combs, stack)

        to_xh0, to_xh1, to_both0, to_both1 = gamma_of(1, (BF, BF, BF, F32))
        via_both, via_xl = flip_x(to_xh0, 3), flip_x(to_xh1, 1)
        from_both0 = flip_x(to_both0, 3)
        mine0, mine1, to_xl0, to_xl1 = gamma_of(0, (F32, F32, F32, BF))
        via_both, via_xl, to_xl1 = lax.optimization_barrier((via_both, via_xl, to_xl1))
        from_xl1 = flip_x(to_xl1, 1)
        from_xl0 = flip_x((to_xl0 + via_both.astype(F32)).astype(BF), 1)
        from_both1 = flip_x((to_both1 + via_xl.astype(F32)).astype(BF), 3)
        first = (mine0 + from_xl0.astype(F32) + from_both0.astype(F32)).astype(BF)
        last = (mine1 + from_xl1.astype(F32) + from_both1.astype(F32)).astype(BF)
        total = [t[k] for t in (first, last) for k in range(NZ // 2)]

    with jax.named_scope("spread"):
        got = [total[0]] + [shift(total[k], "z", k) for k in range(1, NZ)]
        out = pl.pallas_call(
            assemble_kernel,
            out_shape=jax.ShapeDtypeStruct((piece, NZ * 2 * aux), BF),
            in_specs=[vmem] * NZ,
            out_specs=vmem,
            compiler_params=pltpu.CompilerParams(vmem_limit_bytes=16 << 20),
        )(*got)
    return out.reshape(occ_g, piece // occ_g, NZ * 2 * aux)


def solution(mesh):
    split = Mesh(mesh.devices.reshape(NY, NXH, NC, NZ, NXL), ("y", "xh", "core", "z", "xl"))
    placed = (P(GRP, None, SH), P(GRP, None, SH), P(), P())
    return jax.shard_map(on_device, mesh=split, in_specs=placed, out_specs=P(GRP, SH, None), check_vma=False)
```

```python
import functools

import jax
import jax.numpy as jnp
from jax import lax
from jax.experimental import pallas as pl
from jax.experimental.pallas import tpu as pltpu
from jax.sharding import Mesh, PartitionSpec as P

BLK = 128
NY, NXH, NC, NZ, NXL = 4, 2, 2, 8, 2
GRP = ("y", "xh", "core")
SH = ("z", "xl")
X = ("xh", "xl")
BF = jnp.bfloat16
COLUMNS = (0, 1, 3, 2)
F32 = jnp.float32


def flip_x(value, bits):
    return lax.ppermute(value, X, [(i, i ^ bits) for i in range(NXH * NXL)])


def shift(value, axis, steps):
    count = lax.axis_size(axis)
    return lax.ppermute(value, axis, [(i, (i + steps) % count) for i in range(count)])


def flip_core(value):
    return lax.ppermute(value, "core", [(0, 1), (1, 0)])


def dot_t(a, b):
    return lax.dot_general(a, b, (((1,), (1,)), ((), ())), preferred_element_type=F32)


def coulomb_kernel(own, xlf, bof, xh, *refs):
    near, far, (p0, p1, p2, p3, p5, p6, p7), refs = refs[0:3], refs[3:6], refs[6:13], refs[13:]
    send_up, send_down, keep_up, keep_down, stack_out, out, stack, left, sem = refs
    z, xl, c = lax.axis_index("z"), lax.axis_index("xl"), lax.axis_index("core")
    rows, half = own.shape

    def lay(target, row0, col0, piece):
        step = 64

        def body(n, carry):
            rows_at = pl.multiple_of(row0 + n * step, step)
            target[pl.ds(rows_at, step), col0:col0 + half] = piece[pl.ds(pl.multiple_of(n * step, step), step), :]
            return carry

        lax.fori_loop(0, piece.shape[0] // step, body, 0)

    for k, pieces in enumerate((near, far)):
        at = 0
        for piece in pieces:
            lay(stack, at, k * half, piece)
            at += piece.shape[0]
    copy = pltpu.make_async_copy(stack, stack_out, sem)
    copy.start()

    @pl.when(xl == c)
    def _():
        lay(left, 0, 0, own)
        lay(left, 0, half, far[0])
        lay(left, rows, 0, xh)
        lay(left, rows, half, bof)

    @pl.when(xl != c)
    def _():
        lay(left, 0, half, own)
        lay(left, 0, 0, xlf)
        lay(left, rows, half, xh)
        lay(left, rows, 0, bof)

    def block(n, carry):
        e, pair = n // 2, lax.rem(n, 2)
        got = dot_t(
            left[pl.ds(pl.multiple_of(e * rows, 128), rows), :],
            stack[pl.ds(pl.multiple_of(pair * 2 * rows, 128), 2 * rows), :],
        )
        for dd in range(2):
            out[lax.rem(e * NY + pair * 2 + dd + NZ - z, NZ)] = got[:, dd * rows:(dd + 1) * rows]
        return carry

    lax.fori_loop(0, NY, block, 0)
    low, high = slice(0, rows // 2), slice(rows // 2, rows)
    for k, ref in ((0, p0), (1, p1), (2, p2), (6, p6), (7, p7)):
        ref[...] = out[k]
    p3[...], p5[...] = out[3, low, :], out[5, high, :]
    send_up[...], send_down[...] = out[4, low, :].astype(BF), out[4, high, :].astype(BF)
    keep_up[...], keep_down[...] = out[3, high, :].astype(BF), out[5, low, :].astype(BF)
    copy.wait()


def combined_kernel(occ_ref, v_col, v_row, mine, up, down, out, scr):
    y, xh, c, z, xl = (lax.axis_index(n) for n in ("y", "xh", "core", "z", "xl"))
    virt = v_row.shape[1]
    count = mine.shape[0] // virt
    e, d = z // NY, lax.rem(z, NY)
    row_occ = ((y * NXH + lax.rem(xh + e, NXH)) * NC + c) * count
    back = jnp.where(d < 2, d, NY + 1 - d)
    col_occ = ((lax.rem(y + NY - back, NY) * NXH + xh) * NC + xl) * count
    for i in range(count):
        for j in range(count):
            tile = (pl.ds(i * virt, virt), pl.ds(j * virt, virt))
            total = mine[tile] + up[tile].astype(F32) + down[tile].astype(F32)
            row, col = v_col[...] - occ_ref[row_occ + i], v_row[...] - occ_ref[col_occ + j]
            amp = (total / (row + col)).astype(BF).astype(F32)
            comb = 2.0 * amp - amp.T
            for zp in range(NZ):
                for h in range(NXL):
                    at = (zp * NXL + h) * 8
                    scr[h, (zp * count + i) * 8:(zp * count + i + 1) * 8, j * virt:(j + 1) * virt] = comb[at:at + 8]
    for h in range(NXL):
        out[h] = scr[h].astype(BF)


def gamma_kernel(*refs, group):
    combs, stack, outs, (left, scr) = refs[0:9], refs[9], refs[10:-2], refs[-2:]
    half, rows = combs[0].shape[1:]
    z, xl = lax.axis_index("z"), lax.axis_index("xl")
    part = combs[7].shape[1]
    places = [(ref, step, 0) for ref, step in zip(combs[:7], (0, 1, -1, 2, -2, 3, -3))]
    for ref, step, row0 in places + [(combs[7], 4, 0), (combs[8], 4, part)]:
        source = lax.rem(z + NZ - step, NZ)

        @pl.when(source // NY == group)
        def _(ref=ref, source=source, row0=row0):
            cols = pl.ds(pl.multiple_of(lax.rem(source, NY) * rows, 128), rows)
            for fl in range(2):
                at = fl * half + row0
                left[at:at + ref.shape[1], cols] = ref[lax.rem(xl + fl, 2)]

    width = 2 * BLK
    piece = half // NZ

    def columns(n, carry):
        cols = pl.ds(pl.multiple_of(n * width, width), width)
        acc = jnp.dot(left[...], stack[:, cols], preferred_element_type=F32)
        for zp in range(NZ):
            at = lax.rem(zp + NZ - z, NZ)
            scr[0, at, :, cols] = acc[zp * piece:(zp + 1) * piece]
            scr[1, at, :, cols] = acc[half + zp * piece:half + (zp + 1) * piece]
        return carry

    lax.fori_loop(0, stack.shape[1] // width, columns, 0)
    n = NZ // 2
    for fl in range(2):
        for p in range(2):
            outs[2 * fl + p][...] = scr[fl, p * n:(p + 1) * n].astype(outs[2 * fl + p].dtype)


def assemble_kernel(*refs):
    out = refs[-1]
    z, core = lax.axis_index("z"), lax.axis_index("core")
    half = refs[0].shape[1] // 2
    for k in range(NZ):
        source = lax.rem(z + NZ - k, NZ)
        for part in range(2):
            start = pl.multiple_of(source * 2 * half + lax.rem(core + part, 2) * half, 128)
            out[:, pl.ds(start, half)] = refs[k][:, part * half:(part + 1) * half]


def on_device(factors, screen, occ_energy, virt_energy):
    occ_g, virt, aux = factors.shape
    rows = occ_g * virt
    hr = rows // 2
    wide_mask = jnp.repeat(jnp.repeat(screen, BLK, axis=1), BLK, axis=2)
    own = (factors * wide_mask.astype(BF)).reshape(rows, aux)

    with jax.named_scope("gather"):
        j0 = lax.ppermute(own, ("core", "xl"), [(0, 0), (1, 2), (2, 1), (3, 3)])
        bof = flip_x(own, 3)
        xlf = lax.ppermute(own, ("core", "xl"), [(0, 1), (3, 2)])
        j1, j3 = shift(j0, "y", 1), shift(j0, "y", -1)
        f0 = flip_core(j0)
        own_b, f0, xlf = lax.optimization_barrier((own, f0, xlf))
        xh = flip_x(own_b, 2)
        j1, j3, bof = lax.optimization_barrier((j1, j3, bof))
        j2a, j2b = shift(j1[:hr], "y", 1), shift(j3[hr:], "y", -1)
        j2a, j2b, xh = lax.optimization_barrier((j2a, j2b, xh))
        outer = jnp.concatenate([j1, j3])
        outer_far = flip_core(outer)
        inner = jnp.concatenate([j2a, j2b])
        inner_far = flip_core(inner)
        near, far = [j0, outer, inner], [f0, outer_far, inner_far]

    vmem = pl.BlockSpec(memory_space=pltpu.VMEM)
    smem = pl.BlockSpec(memory_space=pltpu.SMEM)
    params = pltpu.CompilerParams(vmem_limit_bytes=48 << 20)

    with jax.named_scope("coulomb"):
        whole, part = jax.ShapeDtypeStruct((rows, rows), F32), jax.ShapeDtypeStruct((hr, rows), F32)
        sent = jax.ShapeDtypeStruct((hr, rows), BF)
        mine, p1, p2, p3, p5, p6, p7, up, down, keep_up, keep_down, stack = pl.pallas_call(
            coulomb_kernel,
            out_shape=[whole, whole, whole, part, part, whole, whole, sent, sent, sent, sent]
            + [jax.ShapeDtypeStruct((NY * rows, 2 * aux), BF)],
            in_specs=[vmem] * 10,
            out_specs=[vmem] * 11 + [pl.BlockSpec(memory_space=pl.ANY)],
            scratch_shapes=[
                pltpu.VMEM((NZ, rows, rows), F32),
                pltpu.VMEM((NY * rows, 2 * aux), BF),
                pltpu.VMEM((2 * rows, 2 * aux), BF),
                pltpu.SemaphoreType.DMA,
            ],
            compiler_params=params,
        )(own, xlf, bof, xh, *near, *far)

    with jax.named_scope("ring"):
        up, down = shift(up, "z", 1), shift(down, "z", -1)
        up = jnp.concatenate([(up.astype(F32) + p3).astype(BF), keep_up])
        down = jnp.concatenate([keep_down, (down.astype(F32) + p5).astype(BF)])
        for from_up, from_down in ((p2, p6), (p1, p7), (None, None)):
            up, down = shift(up, "z", 1), shift(down, "z", -1)
            if from_up is not None:
                up = (up.astype(F32) + from_up).astype(BF)
                down = (down.astype(F32) + from_down).astype(BF)

    with jax.named_scope("combined"):
        comb = pl.pallas_call(
            combined_kernel,
            out_shape=jax.ShapeDtypeStruct((NXL, hr, rows), BF),
            in_specs=[smem] + [vmem] * 5,
            out_specs=vmem,
            scratch_shapes=[pltpu.VMEM((NXL, hr, rows), F32)],
            compiler_params=params,
        )(occ_energy, virt_energy[:, None], virt_energy[None, :], mine, up, down)
        up1, down1 = shift(comb, "z", 1), shift(comb, "z", -1)
        up2, down2 = shift(up1, "z", 1), shift(down1, "z", -1)
        up3, down3 = shift(up2, "z", 1), shift(down2, "z", -1)
        up4, down4 = shift(up3[:, :hr // 2], "z", 1), shift(down3[:, hr // 2:], "z", -1)
        combs = [comb, up1, down1, up2, down2, up3, down3, up4, down4]

    with jax.named_scope("gamma"):
        piece = hr // NZ

        def gamma_of(group, types):
            return pl.pallas_call(
                functools.partial(gamma_kernel, group=group),
                out_shape=[jax.ShapeDtypeStruct((NZ // 2, piece, 2 * aux), t) for t in types],
                in_specs=[vmem] * 10,
                out_specs=[vmem] * 4,
                scratch_shapes=[
                    pltpu.VMEM((2 * hr, NY * rows), BF),
                    pltpu.VMEM((2, NZ, piece, 2 * aux), F32),
                ],
                compiler_params=params,
            )(*combs, stack)

        to_xh0, to_xh1, to_both0, to_both1 = gamma_of(1, (BF, BF, BF, F32))
        via_both, via_xl = flip_x(to_xh0, 3), flip_x(to_xh1, 1)
        from_both0 = flip_x(to_both0, 3)
        mine0, mine1, to_xl0, to_xl1 = gamma_of(0, (F32, F32, F32, BF))
        via_both, via_xl, to_xl1 = lax.optimization_barrier((via_both, via_xl, to_xl1))
        from_xl1 = flip_x(to_xl1, 1)
        from_xl0 = flip_x((to_xl0 + via_both.astype(F32)).astype(BF), 1)
        from_both1 = flip_x((to_both1 + via_xl.astype(F32)).astype(BF), 3)
        first = (mine0 + from_xl0.astype(F32) + from_both0.astype(F32)).astype(BF)
        last = (mine1 + from_xl1.astype(F32) + from_both1.astype(F32)).astype(BF)
        total = [t[k] for t in (first, last) for k in range(NZ // 2)]

    with jax.named_scope("spread"):
        got = [total[0]] + [shift(total[k], "z", k) for k in range(1, NZ)]
        out = pl.pallas_call(
            assemble_kernel,
            out_shape=jax.ShapeDtypeStruct((piece, NZ * 2 * aux), BF),
            in_specs=[vmem] * NZ,
            out_specs=vmem,
            compiler_params=pltpu.CompilerParams(vmem_limit_bytes=16 << 20),
        )(*got)
    return out.reshape(occ_g, piece // occ_g, NZ * 2 * aux)


def solution(mesh):
    split = Mesh(mesh.devices.reshape(NY, NXH, NC, NZ, NXL), ("y", "xh", "core", "z", "xl"))
    placed = (P(GRP, None, SH), P(GRP, None, SH), P(), P())
    return jax.shard_map(on_device, mesh=split, in_specs=placed, out_specs=P(GRP, SH, None), check_vma=False)
```

```python
import functools

import jax
import jax.numpy as jnp
from jax import lax
from jax.experimental import pallas as pl
from jax.experimental.pallas import tpu as pltpu
from jax.sharding import Mesh, PartitionSpec as P

BLK = 128
NY, NXH, NC, NZ, NXL = 4, 2, 2, 8, 2
GRP = ("y", "xh", "core")
SH = ("z", "xl")
X = ("xh", "xl")
BF = jnp.bfloat16
COLUMNS = (0, 1, 3, 2)
F32 = jnp.float32


def flip_x(value, bits):
    return lax.ppermute(value, X, [(i, i ^ bits) for i in range(NXH * NXL)])


def shift(value, axis, steps):
    count = lax.axis_size(axis)
    return lax.ppermute(value, axis, [(i, (i + steps) % count) for i in range(count)])


def flip_core(value):
    return lax.ppermute(value, "core", [(0, 1), (1, 0)])


def dot_t(a, b):
    return lax.dot_general(a, b, (((1,), (1,)), ((), ())), preferred_element_type=F32)


def lay(target, row0, col0, piece):
    step, width = 64, piece.shape[1]

    def body(n, carry):
        rows_at = pl.multiple_of(row0 + n * step, step)
        target[pl.ds(rows_at, step), col0:col0 + width] = piece[pl.ds(pl.multiple_of(n * step, step), step), :]
        return carry

    lax.fori_loop(0, piece.shape[0] // step, body, 0)


def stacked(target, near, far):
    for k, pieces in enumerate((near, far)):
        at = 0
        for piece in pieces:
            lay(target, at, k * piece.shape[1], piece)
            at += piece.shape[0]


def early_kernel(own, xlf, *refs):
    near, far, (out, stack, left) = refs[0:3], refs[3:6], refs[6:9]
    xl, c = lax.axis_index("xl"), lax.axis_index("core")
    rows, half = own.shape
    stacked(stack, near, far)

    @pl.when(xl == c)
    def _():
        lay(left, 0, 0, own)
        lay(left, 0, half, far[0])

    @pl.when(xl != c)
    def _():
        lay(left, 0, half, own)
        lay(left, 0, 0, xlf)

    def block(n, carry):
        out[n] = dot_t(left[...], stack[pl.ds(pl.multiple_of(n * rows, 128), rows), :])
        return carry

    lax.fori_loop(0, NY - 1, block, 0)


def coulomb_kernel(early, left, bof, xh, many, *refs):
    near, far, (p0, p1, p2, p3, p5, p6, p7), refs = refs[0:2], refs[2:4], refs[4:11], refs[11:]
    send_up, send_down, keep_up, keep_down, last, out, flipped = refs
    z, xl, c = lax.axis_index("z"), lax.axis_index("xl"), lax.axis_index("core")
    rows, half = bof.shape
    stacked(last, near, far)

    @pl.when(xl == c)
    def _():
        lay(flipped, 0, 0, xh)
        lay(flipped, 0, half, bof)

    @pl.when(xl != c)
    def _():
        lay(flipped, 0, half, xh)
        lay(flipped, 0, 0, bof)

    def place(e, d):
        return lax.rem(e * NY + d + NZ - z, NZ)

    def block(n, carry):
        out[place(1, n)] = dot_t(flipped[...], many[pl.ds(pl.multiple_of(n * rows, 128), rows), :])
        out[place(0, n)] = early[n]
        return carry

    lax.fori_loop(0, NY - 1, block, 0)

    def end(e, carry):
        @pl.when(e == 0)
        def _():
            out[place(0, NY - 1)] = dot_t(left[...], last[...])

        @pl.when(e == 1)
        def _():
            out[place(1, NY - 1)] = dot_t(flipped[...], last[...])

        return carry

    lax.fori_loop(0, 2, end, 0)
    low, high = slice(0, rows // 2), slice(rows // 2, rows)
    for k, ref in ((0, p0), (1, p1), (2, p2), (6, p6), (7, p7)):
        ref[...] = out[k]
    p3[...], p5[...] = out[3, low, :], out[5, high, :]
    send_up[...], send_down[...] = out[4, low, :].astype(BF), out[4, high, :].astype(BF)
    keep_up[...], keep_down[...] = out[3, high, :].astype(BF), out[5, low, :].astype(BF)


def combined_kernel(occ_ref, v_col, v_row, mine, up, down, out, scr):
    y, xh, c, z, xl = (lax.axis_index(n) for n in ("y", "xh", "core", "z", "xl"))
    virt = v_row.shape[1]
    count = mine.shape[0] // virt
    e, d = z // NY, lax.rem(z, NY)
    row_occ = ((y * NXH + lax.rem(xh + e, NXH)) * NC + c) * count
    back = jnp.where(d < 2, d, NY + 1 - d)
    col_occ = ((lax.rem(y + NY - back, NY) * NXH + xh) * NC + xl) * count
    for i in range(count):
        for j in range(count):
            tile = (pl.ds(i * virt, virt), pl.ds(j * virt, virt))
            total = mine[tile] + up[tile].astype(F32) + down[tile].astype(F32)
            row, col = v_col[...] - occ_ref[row_occ + i], v_row[...] - occ_ref[col_occ + j]
            amp = (total / (row + col)).astype(BF).astype(F32)
            comb = 2.0 * amp - amp.T
            for zp in range(NZ):
                for h in range(NXL):
                    at = (zp * NXL + h) * 8
                    scr[h, (zp * count + i) * 8:(zp * count + i + 1) * 8, j * virt:(j + 1) * virt] = comb[at:at + 8]
    for h in range(NXL):
        out[h] = scr[h].astype(BF)


def gamma_kernel(*refs, group):
    combs, many, last, outs, (left, scr) = refs[0:9], refs[9], refs[10], refs[11:-2], refs[-2:]
    half, rows = combs[0].shape[1:]
    z, xl = lax.axis_index("z"), lax.axis_index("xl")
    part = combs[7].shape[1]
    places = [(ref, step, 0) for ref, step in zip(combs[:7], (0, 1, -1, 2, -2, 3, -3))]
    for ref, step, row0 in places + [(combs[7], 4, 0), (combs[8], 4, part)]:
        source = lax.rem(z + NZ - step, NZ)

        @pl.when(source // NY == group)
        def _(ref=ref, source=source, row0=row0):
            cols = pl.ds(pl.multiple_of(lax.rem(source, NY) * rows, 128), rows)
            for fl in range(2):
                at = fl * half + row0
                left[at:at + ref.shape[1], cols] = ref[lax.rem(xl + fl, 2)]

    width = 2 * BLK
    piece = half // NZ

    def columns(n, carry):
        cols = pl.ds(pl.multiple_of(n * width, width), width)
        acc = jnp.dot(left[:, :many.shape[0]], many[:, cols], preferred_element_type=F32)
        acc += jnp.dot(left[:, many.shape[0]:], last[:, cols], preferred_element_type=F32)
        for zp in range(NZ):
            at = lax.rem(zp + NZ - z, NZ)
            scr[0, at, :, cols] = acc[zp * piece:(zp + 1) * piece]
            scr[1, at, :, cols] = acc[half + zp * piece:half + (zp + 1) * piece]
        return carry

    lax.fori_loop(0, many.shape[1] // width, columns, 0)
    n = NZ // 2
    for fl in range(2):
        for p in range(2):
            outs[2 * fl + p][...] = scr[fl, p * n:(p + 1) * n].astype(outs[2 * fl + p].dtype)


def assemble_kernel(*refs):
    out = refs[-1]
    z, core = lax.axis_index("z"), lax.axis_index("core")
    half = refs[0].shape[1] // 2
    for k in range(NZ):
        source = lax.rem(z + NZ - k, NZ)
        for part in range(2):
            start = pl.multiple_of(source * 2 * half + lax.rem(core + part, 2) * half, 128)
            out[:, pl.ds(start, half)] = refs[k][:, part * half:(part + 1) * half]


def on_device(factors, screen, occ_energy, virt_energy):
    occ_g, virt, aux = factors.shape
    rows = occ_g * virt
    hr = rows // 2
    wide_mask = jnp.repeat(jnp.repeat(screen, BLK, axis=1), BLK, axis=2)
    own = (factors * wide_mask.astype(BF)).reshape(rows, aux)

    with jax.named_scope("gather"):
        j0 = lax.ppermute(own, ("core", "xl"), [(0, 0), (1, 2), (2, 1), (3, 3)])
        bof = flip_x(own, 3)
        xlf = lax.ppermute(own, ("core", "xl"), [(0, 1), (3, 2)])
        j1, j3 = shift(j0, "y", 1), shift(j0, "y", -1)
        f0 = flip_core(j0)
        own_b, f0, xlf = lax.optimization_barrier((own, f0, xlf))
        xh = flip_x(own_b, 2)
        j1, j3, bof = lax.optimization_barrier((j1, j3, bof))
        j2a, j2b = shift(j1[:hr], "y", 1), shift(j3[hr:], "y", -1)
        f1, f3 = flip_core(j1), flip_core(j3)

    vmem = pl.BlockSpec(memory_space=pltpu.VMEM)
    smem = pl.BlockSpec(memory_space=pltpu.SMEM)
    params = pltpu.CompilerParams(vmem_limit_bytes=48 << 20)

    with jax.named_scope("coulomb"):
        whole, part = jax.ShapeDtypeStruct((rows, rows), F32), jax.ShapeDtypeStruct((hr, rows), F32)
        sent = jax.ShapeDtypeStruct((hr, rows), BF)
        early, many, left = pl.pallas_call(
            early_kernel,
            out_shape=[
                jax.ShapeDtypeStruct((NY - 1, rows, rows), F32),
                jax.ShapeDtypeStruct(((NY - 1) * rows, 2 * aux), BF),
                jax.ShapeDtypeStruct((rows, 2 * aux), BF),
            ],
            in_specs=[vmem] * 8,
            out_specs=[vmem] * 3,
            compiler_params=params,
        )(own, xlf, j0, j1, j3, f0, f1, f3)
        early, j2a, j2b, xh = lax.optimization_barrier((early, j2a, j2b, xh))
        f2a, f2b = flip_core(j2a), flip_core(j2b)
        mine, p1, p2, p3, p5, p6, p7, up, down, keep_up, keep_down, last = pl.pallas_call(
            coulomb_kernel,
            out_shape=[whole, whole, whole, part, part, whole, whole, sent, sent, sent, sent]
            + [jax.ShapeDtypeStruct((rows, 2 * aux), BF)],
            in_specs=[vmem] * 9,
            out_specs=[vmem] * 12,
            scratch_shapes=[pltpu.VMEM((NZ, rows, rows), F32), pltpu.VMEM((rows, 2 * aux), BF)],
            compiler_params=params,
        )(early, left, bof, xh, many, j2a, j2b, f2a, f2b)

    with jax.named_scope("ring"):
        up, down = shift(up, "z", 1), shift(down, "z", -1)
        up = jnp.concatenate([(up.astype(F32) + p3).astype(BF), keep_up])
        down = jnp.concatenate([keep_down, (down.astype(F32) + p5).astype(BF)])
        for from_up, from_down in ((p2, p6), (p1, p7), (None, None)):
            up, down = shift(up, "z", 1), shift(down, "z", -1)
            if from_up is not None:
                up = (up.astype(F32) + from_up).astype(BF)
                down = (down.astype(F32) + from_down).astype(BF)

    with jax.named_scope("combined"):
        comb = pl.pallas_call(
            combined_kernel,
            out_shape=jax.ShapeDtypeStruct((NXL, hr, rows), BF),
            in_specs=[smem] + [vmem] * 5,
            out_specs=vmem,
            scratch_shapes=[pltpu.VMEM((NXL, hr, rows), F32)],
            compiler_params=params,
        )(occ_energy, virt_energy[:, None], virt_energy[None, :], mine, up, down)
        up1, down1 = shift(comb, "z", 1), shift(comb, "z", -1)
        up2, down2 = shift(up1, "z", 1), shift(down1, "z", -1)
        up3, down3 = shift(up2, "z", 1), shift(down2, "z", -1)
        up4, down4 = shift(up3[:, :hr // 2], "z", 1), shift(down3[:, hr // 2:], "z", -1)
        combs = [comb, up1, down1, up2, down2, up3, down3, up4, down4]

    with jax.named_scope("gamma"):
        piece = hr // NZ

        def gamma_of(group, types):
            return pl.pallas_call(
                functools.partial(gamma_kernel, group=group),
                out_shape=[jax.ShapeDtypeStruct((NZ // 2, piece, 2 * aux), t) for t in types],
                in_specs=[vmem] * 11,
                out_specs=[vmem] * 4,
                scratch_shapes=[
                    pltpu.VMEM((2 * hr, NY * rows), BF),
                    pltpu.VMEM((2, NZ, piece, 2 * aux), F32),
                ],
                compiler_params=params,
            )(*combs, many, last)

        to_xh0, to_xh1, to_both0, to_both1 = gamma_of(1, (BF, BF, BF, F32))
        via_both, via_xl = flip_x(to_xh0, 3), flip_x(to_xh1, 1)
        from_both0 = flip_x(to_both0, 3)
        mine0, mine1, to_xl0, to_xl1 = gamma_of(0, (F32, F32, F32, BF))
        via_both, via_xl, to_xl1 = lax.optimization_barrier((via_both, via_xl, to_xl1))
        from_xl1 = flip_x(to_xl1, 1)
        from_xl0 = flip_x((to_xl0 + via_both.astype(F32)).astype(BF), 1)
        from_both1 = flip_x((to_both1 + via_xl.astype(F32)).astype(BF), 3)
        first = (mine0 + from_xl0.astype(F32) + from_both0.astype(F32)).astype(BF)
        last = (mine1 + from_xl1.astype(F32) + from_both1.astype(F32)).astype(BF)
        total = [t[k] for t in (first, last) for k in range(NZ // 2)]

    with jax.named_scope("spread"):
        got = [total[0]] + [shift(total[k], "z", k) for k in range(1, NZ)]
        out = pl.pallas_call(
            assemble_kernel,
            out_shape=jax.ShapeDtypeStruct((piece, NZ * 2 * aux), BF),
            in_specs=[vmem] * NZ,
            out_specs=vmem,
            compiler_params=pltpu.CompilerParams(vmem_limit_bytes=16 << 20),
        )(*got)
    return out.reshape(occ_g, piece // occ_g, NZ * 2 * aux)


def solution(mesh):
    split = Mesh(mesh.devices.reshape(NY, NXH, NC, NZ, NXL), ("y", "xh", "core", "z", "xl"))
    placed = (P(GRP, None, SH), P(GRP, None, SH), P(), P())
    return jax.shard_map(on_device, mesh=split, in_specs=placed, out_specs=P(GRP, SH, None), check_vma=False)
```

```python
import functools

import jax
import jax.numpy as jnp
from jax import lax
from jax.experimental import pallas as pl
from jax.experimental.pallas import tpu as pltpu
from jax.sharding import Mesh, PartitionSpec as P

BLK = 128
NY, NXH, NC, NZ, NXL = 4, 2, 2, 8, 2
GRP = ("y", "xh", "core")
SH = ("z", "xl")
X = ("xh", "xl")
BF = jnp.bfloat16
COLUMNS = (0, 1, 3, 2)
F32 = jnp.float32


def flip_x(value, bits):
    return lax.ppermute(value, X, [(i, i ^ bits) for i in range(NXH * NXL)])


def shift(value, axis, steps):
    count = lax.axis_size(axis)
    return lax.ppermute(value, axis, [(i, (i + steps) % count) for i in range(count)])


def flip_core(value):
    return lax.ppermute(value, "core", [(0, 1), (1, 0)])


def dot_t(a, b):
    return lax.dot_general(a, b, (((1,), (1,)), ((), ())), preferred_element_type=F32)


def lay(target, row0, col0, piece):
    step, width = 64, piece.shape[1]

    def body(n, carry):
        rows_at = pl.multiple_of(row0 + n * step, step)
        target[pl.ds(rows_at, step), col0:col0 + width] = piece[pl.ds(pl.multiple_of(n * step, step), step), :]
        return carry

    lax.fori_loop(0, piece.shape[0] // step, body, 0)


def stacked(target, near, far):
    for k, pieces in enumerate((near, far)):
        at = 0
        for piece in pieces:
            lay(target, at, k * piece.shape[1], piece)
            at += piece.shape[0]


def turned(target, row0, piece):
    def body(n, carry):
        tile = piece[:, pl.ds(pl.multiple_of(n * BLK, BLK), BLK)]
        target[pl.ds(pl.multiple_of(row0 + n * BLK, BLK), BLK), :] = tile.T
        return carry

    lax.fori_loop(0, piece.shape[1] // BLK, body, 0)


def early_kernel(own, xlf, bof, *refs):
    near, far, (out, stack, left, bof_turned) = refs[0:3], refs[3:6], refs[6:10]
    xl, c = lax.axis_index("xl"), lax.axis_index("core")
    rows, half = own.shape
    stacked(stack, near, far)
    turned(bof_turned, 0, bof)

    @pl.when(xl == c)
    def _():
        turned(left, 0, own)
        turned(left, half, far[0])

    @pl.when(xl != c)
    def _():
        turned(left, half, own)
        turned(left, 0, xlf)

    def block(n, carry):
        columns = stack[pl.ds(pl.multiple_of(n * rows, 128), rows), :]
        out[n] = jnp.dot(columns, left[...], preferred_element_type=F32)
        return carry

    lax.fori_loop(0, NY - 1, block, 0)


def coulomb_kernel(early, left, bof_turned, xh, many, *refs):
    near, far, (p0, p1, p2, p3, p5, p6, p7), refs = refs[0:2], refs[2:4], refs[4:11], refs[11:]
    send_up, send_down, keep_up, keep_down, last, out, flipped = refs
    z, xl, c = lax.axis_index("z"), lax.axis_index("xl"), lax.axis_index("core")
    rows, half = xh.shape
    stacked(last, near, far)

    @pl.when(xl == c)
    def _():
        turned(flipped, 0, xh)
        lay(flipped, half, 0, bof_turned)

    @pl.when(xl != c)
    def _():
        turned(flipped, half, xh)
        lay(flipped, 0, 0, bof_turned)

    def place(e, d):
        return lax.rem(e * NY + d + NZ - z, NZ)

    def block(n, carry):
        columns = many[pl.ds(pl.multiple_of(n * rows, 128), rows), :]
        out[place(1, n)] = jnp.dot(columns, flipped[...], preferred_element_type=F32)
        out[place(0, n)] = early[n]
        return carry

    lax.fori_loop(0, NY - 1, block, 0)
    out[place(0, NY - 1)] = jnp.dot(last[...], left[...], preferred_element_type=F32)
    out[place(1, NY - 1)] = jnp.dot(last[...], flipped[...], preferred_element_type=F32)
    low, high = slice(0, rows // 2), slice(rows // 2, rows)
    for k, ref in ((0, p0), (1, p1), (2, p2), (6, p6), (7, p7)):
        ref[...] = out[k]
    p3[...], p5[...] = out[3, low, :], out[5, high, :]
    send_up[...], send_down[...] = out[4, low, :].astype(BF), out[4, high, :].astype(BF)
    keep_up[...], keep_down[...] = out[3, high, :].astype(BF), out[5, low, :].astype(BF)


def combined_kernel(occ_ref, v_col, v_row, mine, up, down, out, scr):
    y, xh, c, z, xl = (lax.axis_index(n) for n in ("y", "xh", "core", "z", "xl"))
    virt = v_row.shape[1]
    count = mine.shape[0] // virt
    e, d = z // NY, lax.rem(z, NY)
    row_occ = ((y * NXH + lax.rem(xh + e, NXH)) * NC + c) * count
    back = jnp.where(d < 2, d, NY + 1 - d)
    col_occ = ((lax.rem(y + NY - back, NY) * NXH + xh) * NC + xl) * count
    for i in range(count):
        for j in range(count):
            tile = (pl.ds(j * virt, virt), pl.ds(i * virt, virt))
            total = mine[tile] + up[tile].astype(F32) + down[tile].astype(F32)
            row, col = v_row[...] - occ_ref[row_occ + i], v_col[...] - occ_ref[col_occ + j]
            amp = (total / (row + col)).astype(BF).astype(F32)
            comb = 2.0 * amp.T - amp
            for zp in range(NZ):
                for h in range(NXL):
                    at = (zp * NXL + h) * 8
                    scr[h, (zp * count + i) * 8:(zp * count + i + 1) * 8, j * virt:(j + 1) * virt] = comb[at:at + 8]
    for h in range(NXL):
        out[h] = scr[h].astype(BF)


def gamma_kernel(*refs, group):
    combs, many, last, outs, (left, scr) = refs[0:9], refs[9], refs[10], refs[11:-2], refs[-2:]
    half, rows = combs[0].shape[1:]
    z, xl = lax.axis_index("z"), lax.axis_index("xl")
    part = combs[7].shape[1]
    places = [(ref, step, 0) for ref, step in zip(combs[:7], (0, 1, -1, 2, -2, 3, -3))]
    for ref, step, row0 in places + [(combs[7], 4, 0), (combs[8], 4, part)]:
        source = lax.rem(z + NZ - step, NZ)

        @pl.when(source // NY == group)
        def _(ref=ref, source=source, row0=row0):
            cols = pl.ds(pl.multiple_of(lax.rem(source, NY) * rows, 128), rows)
            for fl in range(2):
                at = fl * half + row0
                left[at:at + ref.shape[1], cols] = ref[lax.rem(xl + fl, 2)]

    width = 2 * BLK
    piece = half // NZ

    def columns(n, carry):
        cols = pl.ds(pl.multiple_of(n * width, width), width)
        acc = jnp.dot(left[:, :many.shape[0]], many[:, cols], preferred_element_type=F32)
        acc += jnp.dot(left[:, many.shape[0]:], last[:, cols], preferred_element_type=F32)
        for zp in range(NZ):
            at = lax.rem(zp + NZ - z, NZ)
            scr[0, at, :, cols] = acc[zp * piece:(zp + 1) * piece]
            scr[1, at, :, cols] = acc[half + zp * piece:half + (zp + 1) * piece]
        return carry

    lax.fori_loop(0, many.shape[1] // width, columns, 0)
    n = NZ // 2
    for fl in range(2):
        for p in range(2):
            outs[2 * fl + p][...] = scr[fl, p * n:(p + 1) * n].astype(outs[2 * fl + p].dtype)


def assemble_kernel(*refs):
    out = refs[-1]
    z, core = lax.axis_index("z"), lax.axis_index("core")
    half = refs[0].shape[1] // 2
    for k in range(NZ):
        source = lax.rem(z + NZ - k, NZ)
        for part in range(2):
            start = pl.multiple_of(source * 2 * half + lax.rem(core + part, 2) * half, 128)
            out[:, pl.ds(start, half)] = refs[k][:, part * half:(part + 1) * half]


def on_device(factors, screen, occ_energy, virt_energy):
    occ_g, virt, aux = factors.shape
    rows = occ_g * virt
    hr = rows // 2
    wide_mask = jnp.repeat(jnp.repeat(screen, BLK, axis=1), BLK, axis=2)
    own = (factors * wide_mask.astype(BF)).reshape(rows, aux)

    with jax.named_scope("gather"):
        j0 = lax.ppermute(own, ("core", "xl"), [(0, 0), (1, 2), (2, 1), (3, 3)])
        bof = flip_x(own, 3)
        xlf = lax.ppermute(own, ("core", "xl"), [(0, 1), (3, 2)])
        j1, j3 = shift(j0, "y", 1), shift(j0, "y", -1)
        f0 = flip_core(j0)
        own_b, f0, xlf = lax.optimization_barrier((own, f0, xlf))
        xh = flip_x(own_b, 2)
        j1, j3, bof = lax.optimization_barrier((j1, j3, bof))
        j2a, j2b = shift(j1[:hr], "y", 1), shift(j3[hr:], "y", -1)
        f1, f3 = flip_core(j1), flip_core(j3)

    vmem = pl.BlockSpec(memory_space=pltpu.VMEM)
    smem = pl.BlockSpec(memory_space=pltpu.SMEM)
    params = pltpu.CompilerParams(vmem_limit_bytes=48 << 20)

    with jax.named_scope("coulomb"):
        whole, part = jax.ShapeDtypeStruct((rows, rows), F32), jax.ShapeDtypeStruct((hr, rows), F32)
        sent = jax.ShapeDtypeStruct((hr, rows), BF)
        early, many, left, bof_turned = pl.pallas_call(
            early_kernel,
            out_shape=[
                jax.ShapeDtypeStruct((NY - 1, rows, rows), F32),
                jax.ShapeDtypeStruct(((NY - 1) * rows, 2 * aux), BF),
                jax.ShapeDtypeStruct((2 * aux, rows), BF),
                jax.ShapeDtypeStruct((aux, rows), BF),
            ],
            in_specs=[vmem] * 9,
            out_specs=[vmem] * 4,
            compiler_params=params,
        )(own, xlf, bof, j0, j1, j3, f0, f1, f3)
        early, j2a, j2b, xh = lax.optimization_barrier((early, j2a, j2b, xh))
        f2a, f2b = flip_core(j2a), flip_core(j2b)
        mine, p1, p2, p3, p5, p6, p7, up, down, keep_up, keep_down, last = pl.pallas_call(
            coulomb_kernel,
            out_shape=[whole, whole, whole, part, part, whole, whole, sent, sent, sent, sent]
            + [jax.ShapeDtypeStruct((rows, 2 * aux), BF)],
            in_specs=[vmem] * 9,
            out_specs=[vmem] * 12,
            scratch_shapes=[pltpu.VMEM((NZ, rows, rows), F32), pltpu.VMEM((2 * aux, rows), BF)],
            compiler_params=params,
        )(early, left, bof_turned, xh, many, j2a, j2b, f2a, f2b)

    with jax.named_scope("ring"):
        up, down = shift(up, "z", 1), shift(down, "z", -1)
        up = jnp.concatenate([(up.astype(F32) + p3).astype(BF), keep_up])
        down = jnp.concatenate([keep_down, (down.astype(F32) + p5).astype(BF)])
        for from_up, from_down in ((p2, p6), (p1, p7), (None, None)):
            up, down = shift(up, "z", 1), shift(down, "z", -1)
            if from_up is not None:
                up = (up.astype(F32) + from_up).astype(BF)
                down = (down.astype(F32) + from_down).astype(BF)

    with jax.named_scope("combined"):
        comb = pl.pallas_call(
            combined_kernel,
            out_shape=jax.ShapeDtypeStruct((NXL, hr, rows), BF),
            in_specs=[smem] + [vmem] * 5,
            out_specs=vmem,
            scratch_shapes=[pltpu.VMEM((NXL, hr, rows), F32)],
            compiler_params=params,
        )(occ_energy, virt_energy[:, None], virt_energy[None, :], mine, up, down)
        up1, down1 = shift(comb, "z", 1), shift(comb, "z", -1)
        up2, down2 = shift(up1, "z", 1), shift(down1, "z", -1)
        up3, down3 = shift(up2, "z", 1), shift(down2, "z", -1)
        up4, down4 = shift(up3[:, :hr // 2], "z", 1), shift(down3[:, hr // 2:], "z", -1)
        combs = [comb, up1, down1, up2, down2, up3, down3, up4, down4]

    with jax.named_scope("gamma"):
        piece = hr // NZ

        def gamma_of(group, types):
            return pl.pallas_call(
                functools.partial(gamma_kernel, group=group),
                out_shape=[jax.ShapeDtypeStruct((NZ // 2, piece, 2 * aux), t) for t in types],
                in_specs=[vmem] * 11,
                out_specs=[vmem] * 4,
                scratch_shapes=[
                    pltpu.VMEM((2 * hr, NY * rows), BF),
                    pltpu.VMEM((2, NZ, piece, 2 * aux), F32),
                ],
                compiler_params=params,
            )(*combs, many, last)

        to_xh0, to_xh1, to_both0, to_both1 = gamma_of(1, (BF, BF, BF, F32))
        via_both, via_xl = flip_x(to_xh0, 3), flip_x(to_xh1, 1)
        from_both0 = flip_x(to_both0, 3)
        mine0, mine1, to_xl0, to_xl1 = gamma_of(0, (F32, F32, F32, BF))
        via_both, via_xl, to_xl1 = lax.optimization_barrier((via_both, via_xl, to_xl1))
        from_xl1 = flip_x(to_xl1, 1)
        from_xl0 = flip_x((to_xl0 + via_both.astype(F32)).astype(BF), 1)
        from_both1 = flip_x((to_both1 + via_xl.astype(F32)).astype(BF), 3)
        first = (mine0 + from_xl0.astype(F32) + from_both0.astype(F32)).astype(BF)
        last = (mine1 + from_xl1.astype(F32) + from_both1.astype(F32)).astype(BF)
        total = [t[k] for t in (first, last) for k in range(NZ // 2)]

    with jax.named_scope("spread"):
        got = [total[0]] + [shift(total[k], "z", k) for k in range(1, NZ)]
        out = pl.pallas_call(
            assemble_kernel,
            out_shape=jax.ShapeDtypeStruct((piece, NZ * 2 * aux), BF),
            in_specs=[vmem] * NZ,
            out_specs=vmem,
            compiler_params=pltpu.CompilerParams(vmem_limit_bytes=16 << 20),
        )(*got)
    return out.reshape(occ_g, piece // occ_g, NZ * 2 * aux)


def solution(mesh):
    split = Mesh(mesh.devices.reshape(NY, NXH, NC, NZ, NXL), ("y", "xh", "core", "z", "xl"))
    placed = (P(GRP, None, SH), P(GRP, None, SH), P(), P())
    return jax.shard_map(on_device, mesh=split, in_specs=placed, out_specs=P(GRP, SH, None), check_vma=False)
```

```python
import functools

import jax
import jax.numpy as jnp
from jax import lax
from jax.experimental import pallas as pl
from jax.experimental.pallas import tpu as pltpu
from jax.sharding import Mesh, PartitionSpec as P

BLK = 128
NY, NXH, NC, NZ, NXL = 4, 2, 2, 8, 2
GRP = ("y", "xh", "core")
SH = ("z", "xl")
X = ("xh", "xl")
BF = jnp.bfloat16
COLUMNS = (0, 1, 3, 2)
F32 = jnp.float32


def flip_x(value, bits):
    return lax.ppermute(value, X, [(i, i ^ bits) for i in range(NXH * NXL)])


def shift(value, axis, steps):
    count = lax.axis_size(axis)
    return lax.ppermute(value, axis, [(i, (i + steps) % count) for i in range(count)])


def flip_core(value):
    return lax.ppermute(value, "core", [(0, 1), (1, 0)])


def dot_t(a, b):
    return lax.dot_general(a, b, (((1,), (1,)), ((), ())), preferred_element_type=F32)


def lay(target, row0, col0, piece):
    step, width = 64, piece.shape[1]

    def body(n, carry):
        rows_at = pl.multiple_of(row0 + n * step, step)
        target[pl.ds(rows_at, step), col0:col0 + width] = piece[pl.ds(pl.multiple_of(n * step, step), step), :]
        return carry

    lax.fori_loop(0, piece.shape[0] // step, body, 0)


def stacked(target, near, far):
    for k, pieces in enumerate((near, far)):
        at = 0
        for piece in pieces:
            lay(target, at, k * piece.shape[1], piece)
            at += piece.shape[0]


def turned(target, row0, piece):
    def body(n, carry):
        tile = piece[:, pl.ds(pl.multiple_of(n * BLK, BLK), BLK)]
        target[pl.ds(pl.multiple_of(row0 + n * BLK, BLK), BLK), :] = tile.T
        return carry

    lax.fori_loop(0, piece.shape[1] // BLK, body, 0)


def early_kernel(own, xlf, bof, *refs):
    near, far, (out, stack, left, bof_turned) = refs[0:3], refs[3:6], refs[6:10]
    xl, c = lax.axis_index("xl"), lax.axis_index("core")
    rows, half = own.shape
    stacked(stack, near, far)
    turned(bof_turned, 0, bof)

    @pl.when(xl == c)
    def _():
        turned(left, 0, own)
        turned(left, half, far[0])

    @pl.when(xl != c)
    def _():
        turned(left, half, own)
        turned(left, 0, xlf)

    def block(n, carry):
        columns = stack[pl.ds(pl.multiple_of(n * rows, 128), rows), :]
        out[n] = jnp.dot(columns, left[...], preferred_element_type=F32)
        return carry

    lax.fori_loop(0, NY - 1, block, 0)


def coulomb_kernel(early, left, bof_turned, xh, many, *refs):
    near, far, (p0, p1, p2, p3, p5, p6, p7), refs = refs[0:2], refs[2:4], refs[4:11], refs[11:]
    send_up, send_down, keep_up, keep_down, last, out, flipped = refs
    z, xl, c = lax.axis_index("z"), lax.axis_index("xl"), lax.axis_index("core")
    rows, half = xh.shape
    stacked(last, near, far)

    @pl.when(xl == c)
    def _():
        turned(flipped, 0, xh)
        lay(flipped, half, 0, bof_turned)

    @pl.when(xl != c)
    def _():
        turned(flipped, half, xh)
        lay(flipped, 0, 0, bof_turned)

    def place(e, d):
        return lax.rem(e * NY + d + NZ - z, NZ)

    def block(n, carry):
        columns = many[pl.ds(pl.multiple_of(n * rows, 128), rows), :]
        out[place(1, n)] = jnp.dot(columns, flipped[...], preferred_element_type=F32)
        out[place(0, n)] = early[n]
        return carry

    lax.fori_loop(0, NY - 1, block, 0)
    out[place(0, NY - 1)] = jnp.dot(last[...], left[...], preferred_element_type=F32)
    out[place(1, NY - 1)] = jnp.dot(last[...], flipped[...], preferred_element_type=F32)
    low, high = slice(0, rows // 2), slice(rows // 2, rows)
    for k, ref in ((0, p0), (1, p1), (2, p2), (6, p6), (7, p7)):
        ref[...] = out[k]
    p3[...], p5[...] = out[3, low, :], out[5, high, :]
    send_up[...], send_down[...] = out[4, low, :].astype(BF), out[4, high, :].astype(BF)
    keep_up[...], keep_down[...] = out[3, high, :].astype(BF), out[5, low, :].astype(BF)


def combined_kernel(occ_ref, v_col, v_row, mine, up, down, out, scr):
    y, xh, c, z, xl = (lax.axis_index(n) for n in ("y", "xh", "core", "z", "xl"))
    virt = v_row.shape[1]
    count = mine.shape[0] // virt
    e, d = z // NY, lax.rem(z, NY)
    row_occ = ((y * NXH + lax.rem(xh + e, NXH)) * NC + c) * count
    back = jnp.where(d < 2, d, NY + 1 - d)
    col_occ = ((lax.rem(y + NY - back, NY) * NXH + xh) * NC + xl) * count
    for i in range(count):
        for j in range(count):
            tile = (pl.ds(j * virt, virt), pl.ds(i * virt, virt))
            total = mine[tile] + up[tile].astype(F32) + down[tile].astype(F32)
            row, col = v_row[...] - occ_ref[row_occ + i], v_col[...] - occ_ref[col_occ + j]
            amp = (total / (row + col)).astype(BF).astype(F32)
            comb = 2.0 * amp.T - amp
            for zp in range(NZ):
                for h in range(NXL):
                    at = (zp * NXL + h) * 8
                    scr[h, (zp * count + i) * 8:(zp * count + i + 1) * 8, j * virt:(j + 1) * virt] = comb[at:at + 8]
    for h in range(NXL):
        out[h] = scr[h].astype(BF)


def gamma_kernel(*refs, group):
    combs, many, last, outs, (left, scr) = refs[0:9], refs[9], refs[10], refs[11:-2], refs[-2:]
    half, rows = combs[0].shape[1:]
    z, xl = lax.axis_index("z"), lax.axis_index("xl")
    part = combs[7].shape[1]
    places = [(ref, step, 0) for ref, step in zip(combs[:7], (0, 1, -1, 2, -2, 3, -3))]
    for ref, step, row0 in places + [(combs[7], 4, 0), (combs[8], 4, part)]:
        source = lax.rem(z + NZ - step, NZ)

        @pl.when(source // NY == group)
        def _(ref=ref, source=source, row0=row0):
            cols = pl.ds(pl.multiple_of(lax.rem(source, NY) * rows, 128), rows)
            for fl in range(2):
                at = fl * half + row0
                left[at:at + ref.shape[1], cols] = ref[lax.rem(xl + fl, 2)]

    width = many.shape[1] // 2
    piece = half // NZ

    def columns(n, carry):
        cols = pl.ds(pl.multiple_of(n * width, BLK), width)
        acc = jnp.dot(left[:, :many.shape[0]], many[:, cols], preferred_element_type=F32)
        acc += jnp.dot(left[:, many.shape[0]:], last[:, cols], preferred_element_type=F32)
        for zp in range(NZ):
            at = lax.rem(zp + NZ - z, NZ)
            scr[0, at, :, cols] = acc[zp * piece:(zp + 1) * piece]
            scr[1, at, :, cols] = acc[half + zp * piece:half + (zp + 1) * piece]
        return carry

    lax.fori_loop(0, many.shape[1] // width, columns, 0)
    n = NZ // 2
    for fl in range(2):
        for p in range(2):
            outs[2 * fl + p][...] = scr[fl, p * n:(p + 1) * n].astype(outs[2 * fl + p].dtype)


def assemble_kernel(*refs):
    out = refs[-1]
    z, core = lax.axis_index("z"), lax.axis_index("core")
    half = refs[0].shape[1] // 2
    for k in range(NZ):
        source = lax.rem(z + NZ - k, NZ)
        for part in range(2):
            start = pl.multiple_of(source * 2 * half + lax.rem(core + part, 2) * half, 128)
            out[:, pl.ds(start, half)] = refs[k][:, part * half:(part + 1) * half]


def on_device(factors, screen, occ_energy, virt_energy):
    occ_g, virt, aux = factors.shape
    rows = occ_g * virt
    hr = rows // 2
    wide_mask = jnp.repeat(jnp.repeat(screen, BLK, axis=1), BLK, axis=2)
    own = (factors * wide_mask.astype(BF)).reshape(rows, aux)

    with jax.named_scope("gather"):
        j0 = lax.ppermute(own, ("core", "xl"), [(0, 0), (1, 2), (2, 1), (3, 3)])
        bof = flip_x(own, 3)
        xlf = lax.ppermute(own, ("core", "xl"), [(0, 1), (3, 2)])
        j1, j3 = shift(j0, "y", 1), shift(j0, "y", -1)
        f0 = flip_core(j0)
        own_b, f0, xlf = lax.optimization_barrier((own, f0, xlf))
        xh = flip_x(own_b, 2)
        j1, j3, bof = lax.optimization_barrier((j1, j3, bof))
        j2a, j2b = shift(j1[:hr], "y", 1), shift(j3[hr:], "y", -1)
        f1, f3 = flip_core(j1), flip_core(j3)

    vmem = pl.BlockSpec(memory_space=pltpu.VMEM)
    smem = pl.BlockSpec(memory_space=pltpu.SMEM)
    params = pltpu.CompilerParams(vmem_limit_bytes=48 << 20)

    with jax.named_scope("coulomb"):
        whole, part = jax.ShapeDtypeStruct((rows, rows), F32), jax.ShapeDtypeStruct((hr, rows), F32)
        sent = jax.ShapeDtypeStruct((hr, rows), BF)
        early, many, left, bof_turned = pl.pallas_call(
            early_kernel,
            out_shape=[
                jax.ShapeDtypeStruct((NY - 1, rows, rows), F32),
                jax.ShapeDtypeStruct(((NY - 1) * rows, 2 * aux), BF),
                jax.ShapeDtypeStruct((2 * aux, rows), BF),
                jax.ShapeDtypeStruct((aux, rows), BF),
            ],
            in_specs=[vmem] * 9,
            out_specs=[vmem] * 4,
            compiler_params=params,
        )(own, xlf, bof, j0, j1, j3, f0, f1, f3)
        early, j2a, j2b = lax.optimization_barrier((early, j2a, j2b))
        f2a, f2b = flip_core(j2a), flip_core(j2b)
        f2a, f2b, xh = lax.optimization_barrier((f2a, f2b, xh))
        mine, p1, p2, p3, p5, p6, p7, up, down, keep_up, keep_down, last = pl.pallas_call(
            coulomb_kernel,
            out_shape=[whole, whole, whole, part, part, whole, whole, sent, sent, sent, sent]
            + [jax.ShapeDtypeStruct((rows, 2 * aux), BF)],
            in_specs=[vmem] * 9,
            out_specs=[vmem] * 12,
            scratch_shapes=[pltpu.VMEM((NZ, rows, rows), F32), pltpu.VMEM((2 * aux, rows), BF)],
            compiler_params=params,
        )(early, left, bof_turned, xh, many, j2a, j2b, f2a, f2b)

    with jax.named_scope("ring"):
        up, down = shift(up, "z", 1), shift(down, "z", -1)
        up = jnp.concatenate([(up.astype(F32) + p3).astype(BF), keep_up])
        down = jnp.concatenate([keep_down, (down.astype(F32) + p5).astype(BF)])
        for from_up, from_down in ((p2, p6), (p1, p7), (None, None)):
            up, down = shift(up, "z", 1), shift(down, "z", -1)
            if from_up is not None:
                up = (up.astype(F32) + from_up).astype(BF)
                down = (down.astype(F32) + from_down).astype(BF)

    with jax.named_scope("combined"):
        comb = pl.pallas_call(
            combined_kernel,
            out_shape=jax.ShapeDtypeStruct((NXL, hr, rows), BF),
            in_specs=[smem] + [vmem] * 5,
            out_specs=vmem,
            scratch_shapes=[pltpu.VMEM((NXL, hr, rows), F32)],
            compiler_params=params,
        )(occ_energy, virt_energy[:, None], virt_energy[None, :], mine, up, down)
        up1, down1 = shift(comb, "z", 1), shift(comb, "z", -1)
        up2, down2 = shift(up1, "z", 1), shift(down1, "z", -1)
        up3, down3 = shift(up2, "z", 1), shift(down2, "z", -1)
        up4, down4 = shift(up3[:, :hr // 2], "z", 1), shift(down3[:, hr // 2:], "z", -1)
        combs = [comb, up1, down1, up2, down2, up3, down3, up4, down4]

    with jax.named_scope("gamma"):
        piece = hr // NZ

        def gamma_of(group, types):
            return pl.pallas_call(
                functools.partial(gamma_kernel, group=group),
                out_shape=[jax.ShapeDtypeStruct((NZ // 2, piece, 2 * aux), t) for t in types],
                in_specs=[vmem] * 11,
                out_specs=[vmem] * 4,
                scratch_shapes=[
                    pltpu.VMEM((2 * hr, NY * rows), BF),
                    pltpu.VMEM((2, NZ, piece, 2 * aux), F32),
                ],
                compiler_params=params,
            )(*combs, many, last)

        to_xh0, to_xh1, to_both0, to_both1 = gamma_of(1, (BF, BF, BF, F32))
        via_both, via_xl = flip_x(to_xh0, 3), flip_x(to_xh1, 1)
        from_both0 = flip_x(to_both0, 3)
        mine0, mine1, to_xl0, to_xl1 = gamma_of(0, (F32, F32, F32, BF))
        via_both, via_xl, to_xl1 = lax.optimization_barrier((via_both, via_xl, to_xl1))
        from_xl1 = flip_x(to_xl1, 1)
        from_xl0 = flip_x((to_xl0 + via_both.astype(F32)).astype(BF), 1)
        from_both1 = flip_x((to_both1 + via_xl.astype(F32)).astype(BF), 3)
        first = (mine0 + from_xl0.astype(F32) + from_both0.astype(F32)).astype(BF)
        last = (mine1 + from_xl1.astype(F32) + from_both1.astype(F32)).astype(BF)
        total = [t[k] for t in (first, last) for k in range(NZ // 2)]

    with jax.named_scope("spread"):
        got = [total[0]] + [shift(total[k], "z", k) for k in range(1, NZ)]
        out = pl.pallas_call(
            assemble_kernel,
            out_shape=jax.ShapeDtypeStruct((piece, NZ * 2 * aux), BF),
            in_specs=[vmem] * NZ,
            out_specs=vmem,
            compiler_params=pltpu.CompilerParams(vmem_limit_bytes=16 << 20),
        )(*got)
    return out.reshape(occ_g, piece // occ_g, NZ * 2 * aux)


def solution(mesh):
    split = Mesh(mesh.devices.reshape(NY, NXH, NC, NZ, NXL), ("y", "xh", "core", "z", "xl"))
    placed = (P(GRP, None, SH), P(GRP, None, SH), P(), P())
    return jax.shard_map(on_device, mesh=split, in_specs=placed, out_specs=P(GRP, SH, None), check_vma=False)
```

```python
import functools

import jax
import jax.numpy as jnp
from jax import lax
from jax.experimental import pallas as pl
from jax.experimental.pallas import tpu as pltpu
from jax.sharding import Mesh, PartitionSpec as P

BLK = 128
NY, NXH, NC, NZ, NXL = 4, 2, 2, 8, 2
GRP = ("y", "xh", "core")
SH = ("z", "xl")
X = ("xh", "xl")
BF = jnp.bfloat16
COLUMNS = (0, 1, 3, 2)
F32 = jnp.float32


def flip_x(value, bits):
    return lax.ppermute(value, X, [(i, i ^ bits) for i in range(NXH * NXL)])


def shift(value, axis, steps):
    count = lax.axis_size(axis)
    return lax.ppermute(value, axis, [(i, (i + steps) % count) for i in range(count)])


def flip_core(value):
    return lax.ppermute(value, "core", [(0, 1), (1, 0)])


def dot_t(a, b):
    return lax.dot_general(a, b, (((1,), (1,)), ((), ())), preferred_element_type=F32)


def lay(target, row0, col0, piece):
    step, width = 64, piece.shape[1]

    def body(n, carry):
        rows_at = pl.multiple_of(row0 + n * step, step)
        target[pl.ds(rows_at, step), col0:col0 + width] = piece[pl.ds(pl.multiple_of(n * step, step), step), :]
        return carry

    lax.fori_loop(0, piece.shape[0] // step, body, 0)


def stacked(target, near, far):
    for k, pieces in enumerate((near, far)):
        at = 0
        for piece in pieces:
            lay(target, at, k * piece.shape[1], piece)
            at += piece.shape[0]


def turned(target, row0, piece):
    def body(n, carry):
        tile = piece[:, pl.ds(pl.multiple_of(n * BLK, BLK), BLK)]
        target[pl.ds(pl.multiple_of(row0 + n * BLK, BLK), BLK), :] = tile.T
        return carry

    lax.fori_loop(0, piece.shape[1] // BLK, body, 0)


def early_kernel(own, xlf, bof, *refs):
    near, far, (out, stack, left, bof_turned) = refs[0:3], refs[3:6], refs[6:10]
    xl, c = lax.axis_index("xl"), lax.axis_index("core")
    rows, half = own.shape
    stacked(stack, near, far)
    turned(bof_turned, 0, bof)

    @pl.when(xl == c)
    def _():
        turned(left, 0, own)
        turned(left, half, far[0])

    @pl.when(xl != c)
    def _():
        turned(left, half, own)
        turned(left, 0, xlf)

    def block(n, carry):
        columns = stack[pl.ds(pl.multiple_of(n * rows, 128), rows), :]
        out[n] = jnp.dot(columns, left[...], preferred_element_type=F32)
        return carry

    lax.fori_loop(0, NY - 1, block, 0)


def coulomb_kernel(early, left, bof_turned, xh, many, *refs):
    near, far, (p0, p1, p2, p3, p5, p6, p7), refs = refs[0:2], refs[2:4], refs[4:11], refs[11:]
    send_up, send_down, keep_up, keep_down, last, out, flipped = refs
    z, xl, c = lax.axis_index("z"), lax.axis_index("xl"), lax.axis_index("core")
    rows, half = xh.shape
    stacked(last, near, far)

    @pl.when(xl == c)
    def _():
        turned(flipped, 0, xh)
        lay(flipped, half, 0, bof_turned)

    @pl.when(xl != c)
    def _():
        turned(flipped, half, xh)
        lay(flipped, 0, 0, bof_turned)

    def place(e, d):
        return lax.rem(e * NY + d + NZ - z, NZ)

    got = jnp.dot(many[...], flipped[...], preferred_element_type=F32)
    for n in range(NY - 1):
        out[place(1, n)] = got[n * rows:(n + 1) * rows]
        out[place(0, n)] = early[n]
    out[place(0, NY - 1)] = jnp.dot(last[...], left[...], preferred_element_type=F32)
    out[place(1, NY - 1)] = jnp.dot(last[...], flipped[...], preferred_element_type=F32)
    low, high = slice(0, rows // 2), slice(rows // 2, rows)
    for k, ref in ((0, p0), (1, p1), (2, p2), (6, p6), (7, p7)):
        ref[...] = out[k]
    p3[...], p5[...] = out[3, low, :], out[5, high, :]
    send_up[...], send_down[...] = out[4, low, :].astype(BF), out[4, high, :].astype(BF)
    keep_up[...], keep_down[...] = out[3, high, :].astype(BF), out[5, low, :].astype(BF)


def combined_kernel(occ_ref, v_col, v_row, mine, up, down, out, scr):
    y, xh, c, z, xl = (lax.axis_index(n) for n in ("y", "xh", "core", "z", "xl"))
    virt = v_row.shape[1]
    count = mine.shape[0] // virt
    e, d = z // NY, lax.rem(z, NY)
    row_occ = ((y * NXH + lax.rem(xh + e, NXH)) * NC + c) * count
    back = jnp.where(d < 2, d, NY + 1 - d)
    col_occ = ((lax.rem(y + NY - back, NY) * NXH + xh) * NC + xl) * count
    for i in range(count):
        for j in range(count):
            tile = (pl.ds(j * virt, virt), pl.ds(i * virt, virt))
            total = mine[tile] + up[tile].astype(F32) + down[tile].astype(F32)
            row, col = v_row[...] - occ_ref[row_occ + i], v_col[...] - occ_ref[col_occ + j]
            amp = (total / (row + col)).astype(BF).astype(F32)
            comb = 2.0 * amp.T - amp
            for zp in range(NZ):
                for h in range(NXL):
                    at = (zp * NXL + h) * 8
                    scr[h, (zp * count + i) * 8:(zp * count + i + 1) * 8, j * virt:(j + 1) * virt] = comb[at:at + 8]
    for h in range(NXL):
        out[h] = scr[h].astype(BF)


def gamma_kernel(*refs, group):
    combs, many, last, outs, (left, scr) = refs[0:9], refs[9], refs[10], refs[11:-2], refs[-2:]
    half, rows = combs[0].shape[1:]
    z, xl = lax.axis_index("z"), lax.axis_index("xl")
    part = combs[7].shape[1]
    places = [(ref, step, 0) for ref, step in zip(combs[:7], (0, 1, -1, 2, -2, 3, -3))]
    for ref, step, row0 in places + [(combs[7], 4, 0), (combs[8], 4, part)]:
        source = lax.rem(z + NZ - step, NZ)

        @pl.when(source // NY == group)
        def _(ref=ref, source=source, row0=row0):
            cols = pl.ds(pl.multiple_of(lax.rem(source, NY) * rows, 128), rows)
            for fl in range(2):
                at = fl * half + row0
                left[at:at + ref.shape[1], cols] = ref[lax.rem(xl + fl, 2)]

    width = 2 * BLK
    piece = half // NZ

    def columns(n, carry):
        cols = pl.ds(pl.multiple_of(n * width, width), width)
        acc = jnp.dot(left[:, :many.shape[0]], many[:, cols], preferred_element_type=F32)
        acc += jnp.dot(left[:, many.shape[0]:], last[:, cols], preferred_element_type=F32)
        for zp in range(NZ):
            at = lax.rem(zp + NZ - z, NZ)
            scr[0, at, :, cols] = acc[zp * piece:(zp + 1) * piece]
            scr[1, at, :, cols] = acc[half + zp * piece:half + (zp + 1) * piece]
        return carry

    lax.fori_loop(0, many.shape[1] // width, columns, 0)
    n = NZ // 2
    for fl in range(2):
        for p in range(2):
            outs[2 * fl + p][...] = scr[fl, p * n:(p + 1) * n].astype(outs[2 * fl + p].dtype)


def assemble_kernel(*refs):
    out = refs[-1]
    z, core = lax.axis_index("z"), lax.axis_index("core")
    half = refs[0].shape[1] // 2
    for k in range(NZ):
        source = lax.rem(z + NZ - k, NZ)
        for part in range(2):
            start = pl.multiple_of(source * 2 * half + lax.rem(core + part, 2) * half, 128)
            out[:, pl.ds(start, half)] = refs[k][:, part * half:(part + 1) * half]


def on_device(factors, screen, occ_energy, virt_energy):
    occ_g, virt, aux = factors.shape
    rows = occ_g * virt
    hr = rows // 2
    wide_mask = jnp.repeat(jnp.repeat(screen, BLK, axis=1), BLK, axis=2)
    own = (factors * wide_mask.astype(BF)).reshape(rows, aux)

    with jax.named_scope("gather"):
        j0 = lax.ppermute(own, ("core", "xl"), [(0, 0), (1, 2), (2, 1), (3, 3)])
        bof = flip_x(own, 3)
        xlf = lax.ppermute(own, ("core", "xl"), [(0, 1), (3, 2)])
        j1, j3 = shift(j0, "y", 1), shift(j0, "y", -1)
        f0 = flip_core(j0)
        own_b, f0, xlf = lax.optimization_barrier((own, f0, xlf))
        xh = flip_x(own_b, 2)
        j1, j3, bof = lax.optimization_barrier((j1, j3, bof))
        j2a, j2b = shift(j1[:hr], "y", 1), shift(j3[hr:], "y", -1)
        f1, f3 = flip_core(j1), flip_core(j3)

    vmem = pl.BlockSpec(memory_space=pltpu.VMEM)
    smem = pl.BlockSpec(memory_space=pltpu.SMEM)
    params = pltpu.CompilerParams(vmem_limit_bytes=48 << 20)

    with jax.named_scope("coulomb"):
        whole, part = jax.ShapeDtypeStruct((rows, rows), F32), jax.ShapeDtypeStruct((hr, rows), F32)
        sent = jax.ShapeDtypeStruct((hr, rows), BF)
        early, many, left, bof_turned = pl.pallas_call(
            early_kernel,
            out_shape=[
                jax.ShapeDtypeStruct((NY - 1, rows, rows), F32),
                jax.ShapeDtypeStruct(((NY - 1) * rows, 2 * aux), BF),
                jax.ShapeDtypeStruct((2 * aux, rows), BF),
                jax.ShapeDtypeStruct((aux, rows), BF),
            ],
            in_specs=[vmem] * 9,
            out_specs=[vmem] * 4,
            compiler_params=params,
        )(own, xlf, bof, j0, j1, j3, f0, f1, f3)
        early, j2a, j2b, xh = lax.optimization_barrier((early, j2a, j2b, xh))
        f2a, f2b = flip_core(j2a), flip_core(j2b)
        mine, p1, p2, p3, p5, p6, p7, up, down, keep_up, keep_down, last = pl.pallas_call(
            coulomb_kernel,
            out_shape=[whole, whole, whole, part, part, whole, whole, sent, sent, sent, sent]
            + [jax.ShapeDtypeStruct((rows, 2 * aux), BF)],
            in_specs=[vmem] * 9,
            out_specs=[vmem] * 12,
            scratch_shapes=[pltpu.VMEM((NZ, rows, rows), F32), pltpu.VMEM((2 * aux, rows), BF)],
            compiler_params=params,
        )(early, left, bof_turned, xh, many, j2a, j2b, f2a, f2b)

    with jax.named_scope("ring"):
        up, down = shift(up, "z", 1), shift(down, "z", -1)
        up = jnp.concatenate([(up.astype(F32) + p3).astype(BF), keep_up])
        down = jnp.concatenate([keep_down, (down.astype(F32) + p5).astype(BF)])
        for from_up, from_down in ((p2, p6), (p1, p7), (None, None)):
            up, down = shift(up, "z", 1), shift(down, "z", -1)
            if from_up is not None:
                up = (up.astype(F32) + from_up).astype(BF)
                down = (down.astype(F32) + from_down).astype(BF)

    with jax.named_scope("combined"):
        comb = pl.pallas_call(
            combined_kernel,
            out_shape=jax.ShapeDtypeStruct((NXL, hr, rows), BF),
            in_specs=[smem] + [vmem] * 5,
            out_specs=vmem,
            scratch_shapes=[pltpu.VMEM((NXL, hr, rows), F32)],
            compiler_params=params,
        )(occ_energy, virt_energy[:, None], virt_energy[None, :], mine, up, down)
        up1, down1 = shift(comb, "z", 1), shift(comb, "z", -1)
        up2, down2 = shift(up1, "z", 1), shift(down1, "z", -1)
        up3, down3 = shift(up2, "z", 1), shift(down2, "z", -1)
        up4, down4 = shift(up3[:, :hr // 2], "z", 1), shift(down3[:, hr // 2:], "z", -1)
        combs = [comb, up1, down1, up2, down2, up3, down3, up4, down4]

    with jax.named_scope("gamma"):
        piece = hr // NZ

        def gamma_of(group, types):
            return pl.pallas_call(
                functools.partial(gamma_kernel, group=group),
                out_shape=[jax.ShapeDtypeStruct((NZ // 2, piece, 2 * aux), t) for t in types],
                in_specs=[vmem] * 11,
                out_specs=[vmem] * 4,
                scratch_shapes=[
                    pltpu.VMEM((2 * hr, NY * rows), BF),
                    pltpu.VMEM((2, NZ, piece, 2 * aux), F32),
                ],
                compiler_params=params,
            )(*combs, many, last)

        to_xh0, to_xh1, to_both0, to_both1 = gamma_of(1, (BF, BF, BF, F32))
        via_both, via_xl = flip_x(to_xh0, 3), flip_x(to_xh1, 1)
        from_both0 = flip_x(to_both0, 3)
        mine0, mine1, to_xl0, to_xl1 = gamma_of(0, (F32, F32, F32, BF))
        via_both, via_xl, to_xl1 = lax.optimization_barrier((via_both, via_xl, to_xl1))
        from_xl1 = flip_x(to_xl1, 1)
        from_xl0 = flip_x((to_xl0 + via_both.astype(F32)).astype(BF), 1)
        from_both1 = flip_x((to_both1 + via_xl.astype(F32)).astype(BF), 3)
        first = (mine0 + from_xl0.astype(F32) + from_both0.astype(F32)).astype(BF)
        last = (mine1 + from_xl1.astype(F32) + from_both1.astype(F32)).astype(BF)
        total = [t[k] for t in (first, last) for k in range(NZ // 2)]

    with jax.named_scope("spread"):
        got = [total[0]] + [shift(total[k], "z", k) for k in range(1, NZ)]
        out = pl.pallas_call(
            assemble_kernel,
            out_shape=jax.ShapeDtypeStruct((piece, NZ * 2 * aux), BF),
            in_specs=[vmem] * NZ,
            out_specs=vmem,
            compiler_params=pltpu.CompilerParams(vmem_limit_bytes=16 << 20),
        )(*got)
    return out.reshape(occ_g, piece // occ_g, NZ * 2 * aux)


def solution(mesh):
    split = Mesh(mesh.devices.reshape(NY, NXH, NC, NZ, NXL), ("y", "xh", "core", "z", "xl"))
    placed = (P(GRP, None, SH), P(GRP, None, SH), P(), P())
    return jax.shard_map(on_device, mesh=split, in_specs=placed, out_specs=P(GRP, SH, None), check_vma=False)
```
